128 devices in a mesh: dp: 16 (over z, x_hi, core), tensor: 8 (over x_lo, y).
Axes of the slice: x: 4 (x_hi: 2, x_lo: 2; x = x_hi * 2 + x_lo), y: 4, z: 4, core: 2. Of those that a mesh axis runs over, the one named last changes fastest.
Arguments:
- inputs: bfloat16 [12288, 2304], P('dp'), may hold values from -6 to 6
- up_pre: bfloat16 [12288, 18432], P('dp', 'tensor'), may hold values from -6 to 6
- gate_act: bfloat16 [12288, 18432], P('dp', 'tensor'), may hold values from -0.75 to 3.6
- out_grad: bfloat16 [12288, 2304], P('dp'), may hold values from -7.6546554 to 7.6546554
- down_weight: bfloat16 [2304, 18432], P('dp', 'tensor'), may hold values from -0.046875 to 0.046875
- noise_up: float32 [2304, 18432], P('dp', 'tensor'), may hold values from -48 to 48
- noise_down: float32 [2304, 18432], P('dp', 'tensor'), may hold values from -48 to 48
Outputs:
- up_update: float32 [2304, 18432], P('dp', 'tensor')
- down_update: float32 [2304, 18432], P('dp', 'tensor')
The draws below stay inside these ranges and needn't reach their ends.
All inputs are finite; a program needn't handle non-finite values.
Results may differ from the reference program's by a relative error of at most 0.015.
Values may be sent and summed in bfloat16 or wider, within the bound.
No kernel may reach another device: no remote copies, remote signals or barrier semaphores. Data moves between devices by JAX's collectives and lax.ppermute only.
A program may use at most 256 MiB of HBM per device.

```python
import math
import jax
import jax.numpy as jnp
from jax import lax

D = 2304
FF = 18432
SEQ = 384
EX_DEV = 2
EXAMPLES = 32
TOKENS = 12288
N_DP = 16


def draw_out_grad(key, part):
    key = jax.random.fold_in(key, 11)
    first, second, third = jax.random.split(key, 3)
    ex_scale = jnp.exp(jax.random.uniform(first, (EXAMPLES, 1, 1), jnp.float32) * math.log(10.0))
    tok_scale = jnp.exp(jax.random.uniform(second, (EXAMPLES, SEQ, 1), jnp.float32, math.log(0.3), math.log(3.0)))
    base = jax.random.truncated_normal(third, -4.0, 4.0, (EXAMPLES, SEQ, D), jnp.float32)
    values = ex_scale * tok_scale * base / math.sqrt(SEQ)
    return values.reshape(TOKENS, D).astype(jnp.bfloat16)


def draw_gate_act(key, part):
    key = jax.random.fold_in(key, 23)
    column = jnp.arange(FF, dtype=jnp.float32) / FF
    ramp = 0.5 + column
    values = jax.random.uniform(key, (TOKENS, FF), jnp.float32, -0.5, 1.5)
    return (ramp[None, :] * values).astype(jnp.bfloat16)


def shard_levels(rng, dims, cuts, least, largest):
    gain, own = 1.0, jax.random.fold_in(rng, 6)
    for position, shards_of in cuts:
        heights = jnp.exp(jax.random.uniform(jax.random.fold_in(own, position), (shards_of,), jnp.float32, least / len(cuts), largest / len(cuts)))
        gain = gain * jnp.repeat(heights, dims[position] // shards_of).reshape([-1 if axis == position else 1 for axis in range(len(dims))])
    return gain


def centred(key, dims, scale, limit, cuts=(), kind=jnp.bfloat16):
    level = shard_levels(key, dims, cuts, -0.22, 0.18) if cuts else 1.0
    drawn = jax.random.normal(key, dims, jnp.float32) * scale * level
    return jnp.minimum(jnp.maximum(drawn, -limit), limit).astype(kind)


def setup_inputs(seed: int = 0) -> dict:
    key_of = jax.random.split(jax.random.key(seed), 8)
    inputs = centred(key_of[0], (TOKENS, D), 1.0, 6.0, ((0, 16),))
    up_pre = centred(key_of[1], (TOKENS, FF), 1.0, 6.0, ((0, 16), (1, 8)))
    gate_act = draw_gate_act(jax.random.fold_in(key_of[7], 71), 0)
    out_grad = draw_out_grad(jax.random.fold_in(key_of[7], 71), 0)
    down_weight = centred(key_of[4], (D, FF), FF ** -0.5, 0.046875, ((0, 16), (1, 8)))
    noise_up = centred(key_of[5], (D, FF), 8.0, 48.0, ((0, 16), (1, 8)), jnp.float32)
    noise_down = centred(key_of[6], (D, FF), 8.0, 48.0, ((0, 16), (1, 8)), jnp.float32)
    return {"inputs": inputs, "up_pre": up_pre, "gate_act": gate_act, "out_grad": out_grad, "down_weight": down_weight, "noise_up": noise_up, "noise_down": noise_down}


def reference(inputs, up_pre, gate_act, out_grad, down_weight, noise_up, noise_down):
    clip_bound = 4.0 * math.sqrt(D * FF)
    group = EX_DEV * SEQ

    def one_group(carry, index):
        acc_up, acc_down = carry
        start = (index * group).astype(jnp.int32)
        x_rows = lax.dynamic_slice_in_dim(inputs, start, group, 0)
        dy_rows = lax.dynamic_slice_in_dim(out_grad, start, group, 0)
        up_rows = lax.dynamic_slice_in_dim(up_pre, start, group, 0)
        gate_rows = lax.dynamic_slice_in_dim(gate_act, start, group, 0)
        hidden = (gate_rows.astype(jnp.float32) * up_rows.astype(jnp.float32)).astype(jnp.bfloat16)
        hidden_grad = jnp.dot(dy_rows, down_weight, preferred_element_type=jnp.float32)
        act_grad = (hidden_grad * gate_rows.astype(jnp.float32)).astype(jnp.bfloat16)
        part_up = jnp.zeros((D, FF), jnp.float32)
        part_down = jnp.zeros((D, FF), jnp.float32)
        for example in range(EX_DEV):
            low = example * SEQ
            dy_ex = dy_rows[low:low + SEQ]
            x_ex = x_rows[low:low + SEQ]
            down_part = jnp.dot(dy_ex.T, hidden[low:low + SEQ], preferred_element_type=jnp.float32)
            up_part = jnp.dot(x_ex.T, act_grad[low:low + SEQ], preferred_element_type=jnp.float32)
            sq_norm = jnp.sum(down_part * down_part) + jnp.sum(up_part * up_part)
            clip = clip_bound / jnp.maximum(jnp.sqrt(sq_norm), clip_bound)
            part_up = part_up + clip * up_part
            part_down = part_down + clip * down_part
        acc_up = acc_up + lax.optimization_barrier(part_up.astype(jnp.bfloat16)).astype(jnp.float32)
        acc_down = acc_down + lax.optimization_barrier(part_down.astype(jnp.bfloat16)).astype(jnp.float32)
        return ((acc_up, acc_down), None)
    start_acc = (jnp.zeros((D, FF), jnp.float32), jnp.zeros((D, FF), jnp.float32))
    (acc_up, acc_down), _ = lax.scan(one_group, start_acc, jnp.arange(N_DP, dtype=jnp.int32))
    return ((acc_up + noise_up) / EXAMPLES, (acc_down + noise_down) / EXAMPLES)
```

```python
import math

import jax
import jax.numpy as jnp
from jax import lax
from jax.experimental import pallas as pl
from jax.experimental.pallas import tpu as pltpu
from jax.sharding import PartitionSpec as P

D = 2304
FF = 18432
SEQ = 384
N_DP = 16
N_TENSOR = 8
MIB = 1 << 20

Z_UP = [(i, (i + 4) % 16) for i in range(16)]
Z_DOWN = [(i, (i + 12) % 16) for i in range(16)]
X_SWAP = [(i, i ^ 2) for i in range(16)]
CORE_SWAP = [(i, i ^ 1) for i in range(16)]
Y_TURNS = [[(t, (t & 4) | ((t + k) & 3)) for t in range(8)] for k in (1, 2, 3)]
XLO_SWAP = [(t, t ^ 4) for t in range(8)]


def nt(a, b):
    return lax.dot_general(a, b, (((1,), (1,)), ((), ())), preferred_element_type=jnp.float32)


def nn(a, b):
    return lax.dot_general(a, b, (((1,), (0,)), ((), ())), preferred_element_type=jnp.float32)


def prep_kernel(half_ref, x_ref, dy_ref, gate_ref, up_ref, hid_ref, xt_ref, dyt_ref, gx_ref, vd_ref):
    del half_ref
    hid = (gate_ref[...].astype(jnp.float32) * up_ref[...].astype(jnp.float32)).astype(jnp.bfloat16)
    hid_ref[...] = hid
    x, dy = x_ref[...], dy_ref[...]
    xt_ref[...] = x.T
    dyt_ref[...] = dy.T
    gx_ref[0] = nt(x, x)
    vd_ref[...] = jnp.sum(nt(dy, dy) * nt(hid, hid), axis=0, keepdims=True)[None]


def prep(half, x, dy, gate, up):
    width, ff = x.shape[1], 1152
    split = gate.shape[1] // ff

    def col(i, h):
        return (i, h[0] if split > 1 else 0)

    return pl.pallas_call(
        prep_kernel,
        grid_spec=pltpu.PrefetchScalarGridSpec(
            num_scalar_prefetch=1,
            grid=(2,),
            in_specs=[
                pl.BlockSpec((SEQ, width), lambda i, h: (i, 0)),
                pl.BlockSpec((SEQ, width), lambda i, h: (i, 0)),
                pl.BlockSpec((SEQ, ff), col),
                pl.BlockSpec((SEQ, ff), col),
            ],
            out_specs=[
                pl.BlockSpec((SEQ, ff), lambda i, h: (i, 0)),
                pl.BlockSpec((width, SEQ), lambda i, h: (0, i)),
                pl.BlockSpec((width, SEQ), lambda i, h: (0, i)),
                pl.BlockSpec((1, SEQ, SEQ), lambda i, h: (i, 0, 0)),
                pl.BlockSpec((1, 1, SEQ), lambda i, h: (i, 0, 0)),
            ],
        ),
        out_shape=[
            jax.ShapeDtypeStruct((2 * SEQ, ff), jnp.bfloat16),
            jax.ShapeDtypeStruct((width, 2 * SEQ), jnp.bfloat16),
            jax.ShapeDtypeStruct((width, 2 * SEQ), jnp.bfloat16),
            jax.ShapeDtypeStruct((2, SEQ, SEQ), jnp.float32),
            jax.ShapeDtypeStruct((2, 1, SEQ), jnp.float32),
        ],
        compiler_params=pltpu.CompilerParams(vmem_limit_bytes=40 * MIB),
        cost_estimate=pl.CostEstimate(flops=7_000_000_000, bytes_accessed=20_000_000, transcendentals=0),
        name="prep",
    )(half, x, dy, gate, up)


N_PIECES = 9


def act_kernel(rows_ref, dya_ref, dyb_ref, ga_ref, gb_ref, gxa_ref, gxb_ref, *rest):
    pieces = rest[:N_PIECES]
    act_ref, vu_ref, w_ref, sems = rest[N_PIECES:]
    i = pl.program_id(0)

    @pl.when(i == 0)
    def _():
        copies = []
        for j, piece in enumerate(pieces):
            n = piece.shape[0]
            at = pl.multiple_of(rows_ref[j], 16)
            copies.append(pltpu.make_async_copy(piece, w_ref.at[pl.ds(at, n), :], sems.at[j]))
        for copy in copies:
            copy.start()
        for copy in copies:
            copy.wait()

    def example(dy_ref, gate_ref, gx_ref):
        grad = nn(dy_ref[...], w_ref[...])
        act = (grad * gate_ref[...].astype(jnp.float32)).astype(jnp.bfloat16)
        act_ref[...] = act
        vu_ref[...] = jnp.sum(gx_ref[0] * nt(act, act), axis=0, keepdims=True)[None]

    @pl.when(i < 2)
    def _():
        example(dya_ref, ga_ref, gxa_ref)

    @pl.when(i >= 2)
    def _():
        example(dyb_ref, gb_ref, gxb_ref)


def act_grads(scalars, dy_a, dy_b, gate_a, gate_b, gx_a, gx_b, pieces):
    width, ff = dy_a.shape[1], 1152

    def first(i, s):
        return jnp.minimum(i, 1)

    def second(i, s):
        return jnp.maximum(i - 2, 0)

    return pl.pallas_call(
        act_kernel,
        grid_spec=pltpu.PrefetchScalarGridSpec(
            num_scalar_prefetch=1,
            grid=(4,),
            in_specs=[
                pl.BlockSpec((SEQ, width), lambda i, s: (first(i, s), 0)),
                pl.BlockSpec((SEQ, width), lambda i, s: (second(i, s), 0)),
                pl.BlockSpec((SEQ, ff), lambda i, s: (first(i, s), s[N_PIECES])),
                pl.BlockSpec((SEQ, ff), lambda i, s: (second(i, s), 0)),
                pl.BlockSpec((1, SEQ, SEQ), lambda i, s: (first(i, s), 0, 0)),
                pl.BlockSpec((1, SEQ, SEQ), lambda i, s: (second(i, s), 0, 0)),
            ]
            + [pl.BlockSpec(memory_space=pl.ANY)] * N_PIECES,
            out_specs=[
                pl.BlockSpec((SEQ, ff), lambda i, s: (i, 0)),
                pl.BlockSpec((1, 1, SEQ), lambda i, s: (i, 0, 0)),
            ],
            scratch_shapes=[pltpu.VMEM((width, ff), jnp.bfloat16), pltpu.SemaphoreType.DMA((N_PIECES,))],
        ),
        out_shape=[
            jax.ShapeDtypeStruct((4 * SEQ, ff), jnp.bfloat16),
            jax.ShapeDtypeStruct((4, 1, SEQ), jnp.float32),
        ],
        compiler_params=pltpu.CompilerParams(vmem_limit_bytes=40 * MIB),
        cost_estimate=pl.CostEstimate(flops=10_000_000_000, bytes_accessed=25_000_000, transcendentals=0),
        name="act_grads",
    )(scalars, dy_a, dy_b, gate_a, gate_b, gx_a, gx_b, *pieces)


def share_kernel(chunk_ref, clip_ref, la_ref, lb_ref, ra_ref, rb_ref, out_ref, sa_ref, sb_ref):
    del chunk_ref

    @pl.when(pl.program_id(0) == 0)
    def _():
        for e in range(2):
            rows = pl.ds(e * SEQ, SEQ)
            sa_ref[rows, :] = (ra_ref[rows, :].astype(jnp.float32) * clip_ref[e]).astype(jnp.bfloat16)
            sb_ref[rows, :] = (rb_ref[rows, :].astype(jnp.float32) * clip_ref[2 + e]).astype(jnp.bfloat16)

    out_ref[0] = (nn(la_ref[...], sa_ref[...]) + nn(lb_ref[...], sb_ref[...])).astype(out_ref.dtype)


def shares(chunks, clip, lhs_a, lhs_b, rhs_a, rhs_b, b_block, rows, dtype, name):
    n, ff, tok = chunks.shape[0], rhs_a.shape[1], 2 * SEQ
    return pl.pallas_call(
        share_kernel,
        grid_spec=pltpu.PrefetchScalarGridSpec(
            num_scalar_prefetch=2,
            grid=(n,),
            in_specs=[
                pl.BlockSpec((rows, tok), lambda i, s, c: (s[i], 0)),
                pl.BlockSpec((rows, tok), lambda i, s, c: (s[i], 0)),
                pl.BlockSpec((tok, ff), lambda i, s, c: (0, 0)),
                pl.BlockSpec((tok, ff), lambda i, s, c: (b_block, 0)),
            ],
            out_specs=pl.BlockSpec((1, rows, ff), lambda i, s, c: (i, 0, 0)),
            scratch_shapes=[pltpu.VMEM((tok, ff), jnp.bfloat16)] * 2,
        ),
        out_shape=jax.ShapeDtypeStruct((n, rows, ff), dtype),
        compiler_params=pltpu.CompilerParams(vmem_limit_bytes=40 * MIB),
        cost_estimate=pl.CostEstimate(flops=n * 1_020_000_000, bytes_accessed=15_000_000, transcendentals=0),
        name=name,
    )(chunks, clip, lhs_a, lhs_b, rhs_a, rhs_b)


def on_device(inputs, up_pre, gate_act, out_grad, down_weight, noise_up, noise_down):
    f32, bf16 = jnp.float32, jnp.bfloat16
    width, local_ff = inputs.shape[1], up_pre.shape[1]
    ff = local_ff // 2
    own_rows = down_weight.shape[0]
    rows = 2 * own_rows
    me = lax.axis_index("dp")
    core, x, z = me % 2, (me // 2) % 2, me // 4

    def chip(dz, dx):
        return ((z + dz) % 4) * 2 + ((x + dx) % 2)

    def half_cols(a, which):
        return lax.dynamic_slice(a, (0, which * ff), (a.shape[0], ff))

    def go(a, perm):
        return lax.ppermute(a, "dp", perm)

    w_mine = half_cols(down_weight, core)
    w_other = go(half_cols(down_weight, 1 - core), CORE_SWAP)
    own = jnp.where(core == 0, jnp.concatenate([w_mine, w_other]), jnp.concatenate([w_other, w_mine]))
    w_zm = go(own, Z_UP)
    w_zp = go(own, Z_DOWN)
    w_x = go(own, X_SWAP)
    w_z2_top = go(w_zm[:own_rows], Z_UP)
    w_z2_bot = go(w_zp[own_rows:], Z_DOWN)
    w_zm_x = go(w_x, Z_UP)
    w_zp_x = go(w_x, Z_DOWN)
    w_z2_x = go(jnp.concatenate([w_z2_top, w_z2_bot]), X_SWAP)
    pieces = [own, w_zm, w_zp, w_x, w_z2_top, w_z2_bot, w_zm_x, w_zp_x, w_z2_x]
    places = [
        chip(0, 0) * rows,
        chip(3, 0) * rows,
        chip(1, 0) * rows,
        chip(0, 1) * rows,
        chip(2, 0) * rows,
        chip(2, 0) * rows + own_rows,
        chip(3, 1) * rows,
        chip(1, 1) * rows,
        chip(2, 1) * rows,
    ]

    dy_b = go(out_grad, CORE_SWAP)
    x_b = go(inputs, CORE_SWAP)
    gate_b = go(half_cols(gate_act, 1 - core), CORE_SWAP)
    up_b = go(half_cols(up_pre, 1 - core), CORE_SWAP)

    half = jnp.stack([core]).astype(jnp.int32)
    hid_a, xt_a, dyt_a, gx_a, vd_a = prep(half, inputs, out_grad, gate_act, up_pre)
    hid_b, xt_b, dyt_b, gx_b, vd_b = prep(half, x_b, dy_b, gate_b, up_b)

    scalars = jnp.stack(places + [core]).astype(jnp.int32)
    act, vu = act_grads(scalars, out_grad, dy_b, gate_act, gate_b, gx_a, gx_b, pieces)

    part = jnp.sum(jnp.concatenate([vd_a, vd_b]) + vu, axis=(1, 2))
    part = part + jnp.roll(lax.ppermute(part, "dp", CORE_SWAP), 2)
    part = part + lax.ppermute(part, "tensor", XLO_SWAP)
    turns = [lax.ppermute(part, "tensor", perm) for perm in Y_TURNS]
    sq_norm = jnp.maximum(part + (turns[0] + turns[2]) + turns[1], 0.0)
    clip_bound = 4.0 * math.sqrt(D * FF)
    clip = clip_bound / jnp.maximum(jnp.sqrt(sq_norm), clip_bound)

    early = jnp.stack([chip(2, 1), chip(1, 1), chip(3, 1)]).astype(jnp.int32)
    late = jnp.stack([chip(2, 0), chip(0, 1), chip(1, 0), chip(3, 0), chip(0, 0)]).astype(jnp.int32)

    def first_part(lhs_a, lhs_b, rhs_a, rhs_b, b_block, name):
        out = shares(early, clip, lhs_a, lhs_b, rhs_a, rhs_b, b_block, rows, bf16, name)
        return go(out[0], X_SWAP), go(out[1], Z_UP), go(out[2], Z_DOWN)

    def second_part(lhs_a, lhs_b, rhs_a, rhs_b, b_block, name):
        return shares(late, clip, lhs_a, lhs_b, rhs_a, rhs_b, b_block, rows, f32, name)

    def reduce_on(got, mine):
        r1, r2p, r2m = got
        s3 = (mine[0] + r1.astype(f32)).astype(bf16)
        r3p = go(s3[:own_rows], Z_UP)
        r3m = go(s3[own_rows:], Z_DOWN)
        s4 = (mine[1] + r2p.astype(f32) + r2m.astype(f32)).astype(bf16)
        r4 = go(s4, X_SWAP)
        s5p = jnp.concatenate([mine[2, :own_rows] + r3p.astype(f32), mine[2, own_rows:]]).astype(bf16)
        s5m = jnp.concatenate([mine[3, :own_rows], mine[3, own_rows:] + r3m.astype(f32)]).astype(bf16)
        r5p = go(s5p, Z_UP)
        r5m = go(s5m, Z_DOWN)
        return mine[4] + r4.astype(f32) + r5p.astype(f32) + r5m.astype(f32)

    down_args = (dyt_a, dyt_b, hid_a, hid_b, 0)
    up_args = (xt_a, xt_b, act, act, 1)
    got_down = first_part(*down_args, "down_first")
    got_up = first_part(*up_args, "up_first")
    mine_down = second_part(*down_args, "down_second")
    mine_up = second_part(*up_args, "up_second")
    sum_down = reduce_on(got_down, mine_down)
    sum_up = reduce_on(got_up, mine_up)

    def finish(total, noise):
        mine = lax.dynamic_slice(total, (core * own_rows, 0), (own_rows, ff))
        other = go(lax.dynamic_slice(total, ((1 - core) * own_rows, 0), (own_rows, ff)), CORE_SWAP)
        whole = jnp.where(
            core == 0, jnp.concatenate([mine, other], axis=1), jnp.concatenate([other, mine], axis=1)
        )
        return (whole + noise) / (2 * N_DP)

    down_update = finish(sum_down, noise_down)
    up_update = finish(sum_up, noise_up)
    return (up_update, down_update)


def solution(mesh):
    in_specs = (
        P("dp", None),
        P("dp", "tensor"),
        P("dp", "tensor"),
        P("dp", None),
        P("dp", "tensor"),
        P("dp", "tensor"),
        P("dp", "tensor"),
    )
    out_specs = (P("dp", "tensor"), P("dp", "tensor"))
    return jax.shard_map(
        on_device, mesh=mesh, in_specs=in_specs, out_specs=out_specs, check_vma=False
    )
```

```python
import functools
import math

import jax
import jax.numpy as jnp
from jax import lax
from jax.experimental import pallas as pl
from jax.experimental.pallas import tpu as pltpu
from jax.sharding import PartitionSpec as P

D = 2304
FF = 18432
SEQ = 384
N_DP = 16
N_TENSOR = 8
COST = pl.CostEstimate(flops=1000, bytes_accessed=1000, transcendentals=0)

Z_UP = [(i, (i + 4) % 16) for i in range(16)]
Z_DOWN = [(i, (i + 12) % 16) for i in range(16)]
X_SWAP = [(i, i ^ 2) for i in range(16)]
CORE_SWAP = [(i, i ^ 1) for i in range(16)]
TENSOR_SWAPS = [[(t, t ^ k) for t in range(8)] for k in (4, 1, 3)]


VMEM = pl.BlockSpec(memory_space=pltpu.VMEM)
SMEM = pl.BlockSpec(memory_space=pltpu.SMEM)
HBM = pl.BlockSpec(memory_space=pl.ANY)


def in_vmem(a):
    return pltpu.with_memory_space_constraint(a, pltpu.VMEM)


def in_hbm(a):
    return pltpu.with_memory_space_constraint(a, pltpu.HBM)


def nt(a, b):
    return lax.dot_general(a, b, (((1,), (1,)), ((), ())), preferred_element_type=jnp.float32)


def nn(a, b):
    return lax.dot_general(a, b, (((1,), (0,)), ((), ())), preferred_element_type=jnp.float32)


def tn(a, b):
    return lax.dot_general(a, b, (((0,), (0,)), ((), ())), preferred_element_type=jnp.float32)


def call(kernel, name, in_specs, out_specs, out_shape, scratch=(), mib=28):
    return pl.pallas_call(
        kernel,
        in_specs=in_specs,
        out_specs=out_specs,
        out_shape=out_shape,
        scratch_shapes=list(scratch),
        compiler_params=pltpu.CompilerParams(vmem_limit_bytes=mib << 20),
        cost_estimate=COST,
        name=name,
    )


def rows_of(e):
    return pl.ds(e * SEQ, SEQ)


def chunk(s_ref, j, ref):
    rows = ref.shape[0] // 8
    return pl.ds(pl.multiple_of(s_ref[j] * rows, 32), rows)


def turn(x_ref, dy_ref, dyt_ref, gx_ref, gdy_ref, arrivals):
    for e in range(2):
        arrivals[2 * e].wait()
        x = x_ref[rows_of(e), :]
        gx_ref[e] = nt(x, x)
        arrivals[2 * e + 1].wait()
        dy = dy_ref[rows_of(e), :]
        dyt_ref[:, rows_of(e)] = dy.T
        gdy_ref[e] = nt(dy, dy)


def token_copies(x_hbm, dy_hbm, x_ref, dy_ref, sems):
    pairs = []
    for e in range(2):
        for src, dst in ((x_hbm, x_ref), (dy_hbm, dy_ref)):
            pairs.append((src.at[rows_of(e), :], dst.at[rows_of(e), :]))
    return [pltpu.make_async_copy(src, dst, sems.at[j]) for j, (src, dst) in enumerate(pairs)]


def hidden_norm(gate_ref, up_ref, gdy_ref, hid_ref, vd_ref):
    at = lax.broadcasted_iota(jnp.int32, vd_ref.shape, 0)
    value = jnp.zeros(vd_ref.shape, jnp.float32)
    for e in range(2):
        gate, up = gate_ref[rows_of(e), :].astype(jnp.float32), up_ref[rows_of(e), :].astype(jnp.float32)
        hid = (gate * up).astype(jnp.bfloat16)
        hid_ref[rows_of(e), :] = hid
        value += jnp.where(at == e, jnp.sum(gdy_ref[e] * nt(hid, hid)), 0.0)
    vd_ref[...] = value


def own_kernel(
    s_ref, x_hbm, dy_hbm, gate_hbm, up_hbm, dyt_ref, gx_hbm, gate_ref, hid_ref, vd_ref, sent_ref,
    x_ref, dy_ref, up_ref, gx_ref, gdy_ref, sems,
):
    tok, ff = hid_ref.shape
    tokens = token_copies(x_hbm, dy_hbm, x_ref, dy_ref, sems)
    mine = pl.ds(pl.multiple_of(s_ref[8] * ff, 128), ff)
    other = pl.ds(pl.multiple_of((1 - s_ref[8]) * ff, 128), ff)
    pairs = [
        (gate_hbm.at[:, mine], gate_ref),
        (up_hbm.at[:, mine], up_ref),
        (gate_hbm.at[:, other], sent_ref.at[pl.ds(0, tok), :]),
        (up_hbm.at[:, other], sent_ref.at[pl.ds(tok, tok), :]),
    ]
    columns = [pltpu.make_async_copy(src, dst, sems.at[4 + j]) for j, (src, dst) in enumerate(pairs)]
    for copy in tokens + columns:
        copy.start()
    turn(x_ref, dy_ref, dyt_ref, gx_ref, gdy_ref, tokens)
    keep = pltpu.make_async_copy(gx_ref, gx_hbm, sems.at[8])
    keep.start()
    columns[0].wait()
    columns[1].wait()
    hidden_norm(gate_ref, up_ref, gdy_ref, hid_ref, vd_ref)
    for copy in columns[2:] + [keep]:
        copy.wait()


def prep_own(scalars, x, dy, gate, up, ff):
    tok, width = x.shape
    bf16, f32 = jnp.bfloat16, jnp.float32
    cols = pltpu.VMEM((tok, ff), bf16)
    gram = (2, SEQ, SEQ)
    return call(
        own_kernel,
        "prep_own",
        [SMEM] + [HBM] * 4,
        [VMEM, HBM] + [VMEM] * 4,
        [
            pltpu.VMEM((width, tok), bf16),
            pltpu.HBM(gram, f32),
            cols,
            cols,
            jax.ShapeDtypeStruct((8, 128), f32),
            pltpu.VMEM((2 * tok, ff), bf16),
        ],
        [pltpu.VMEM((tok, width), bf16)] * 2
        + [cols, pltpu.VMEM(gram, f32), pltpu.VMEM(gram, f32), pltpu.SemaphoreType.DMA((9,))],
    )(scalars, *[in_hbm(a) for a in (x, dy, gate, up)])


def other_kernel(x_hbm, dy_hbm, dyt_ref, gx_hbm, gdy_ref, x_ref, dy_ref, gx_ref, sems):
    tokens = token_copies(x_hbm, dy_hbm, x_ref, dy_ref, sems)
    for copy in tokens:
        copy.start()
    turn(x_ref, dy_ref, dyt_ref, gx_ref, gdy_ref, tokens)
    keep = pltpu.make_async_copy(gx_ref, gx_hbm, sems.at[4])
    keep.start()
    keep.wait()


def prep_other(x, dy):
    tok, width = x.shape
    bf16, f32 = jnp.bfloat16, jnp.float32
    gram = (2, SEQ, SEQ)
    return call(
        other_kernel,
        "prep_other",
        [HBM] * 2,
        [VMEM, HBM, VMEM],
        [pltpu.VMEM((width, tok), bf16), pltpu.HBM(gram, f32), pltpu.VMEM(gram, f32)],
        [pltpu.VMEM((tok, width), bf16)] * 2 + [pltpu.VMEM(gram, f32), pltpu.SemaphoreType.DMA((5,))],
    )(in_hbm(x), in_hbm(dy))


def hidden_kernel(gu_ref, gdy_ref, hid_ref, vd_ref):
    tok = hid_ref.shape[0]
    hidden_norm(gu_ref.at[pl.ds(0, tok), :], gu_ref.at[pl.ds(tok, tok), :], gdy_ref, hid_ref, vd_ref)


def hidden_other(gu, gdy):
    tok, ff = gu.shape[0] // 2, gu.shape[1]
    return call(
        hidden_kernel,
        "hidden_other",
        [VMEM] * 2,
        [VMEM] * 2,
        [pltpu.VMEM((tok, ff), jnp.bfloat16), jax.ShapeDtypeStruct((8, 128), jnp.float32)],
    )(in_vmem(gu), in_vmem(gdy))


def halves_kernel(a_ref, b_ref, top_ref, bottom_ref, sems):
    half = top_ref.shape[0]
    copies = [
        pltpu.make_async_copy(a_ref.at[pl.ds(0, half), :], top_ref, sems.at[0]),
        pltpu.make_async_copy(b_ref.at[pl.ds(half, half), :], bottom_ref, sems.at[1]),
    ]
    for copy in copies:
        copy.start()
    for copy in copies:
        copy.wait()


def halves(a, b):
    half = pltpu.VMEM((a.shape[0] // 2, a.shape[1]), a.dtype)
    return call(halves_kernel, "halves", [HBM] * 2, [VMEM] * 2, [half, half], [pltpu.SemaphoreType.DMA((2,))])(
        in_hbm(a), in_hbm(b)
    )


def fetch(pieces, w_ref, sems):
    copies, at = [], 0
    for j, piece in enumerate(pieces):
        n = piece.shape[0]
        copies.append(pltpu.make_async_copy(piece, w_ref.at[pl.ds(at, n), :], sems.at[j]))
        at += n
    for copy in copies:
        copy.start()
    for copy in copies:
        copy.wait()


def chunks_of(s_ref, first, n, ref, columns):
    return jnp.concatenate([ref[chunk(s_ref, j, ref), columns] for j in range(first, first + n)])


def near_kernel(n, s_ref, dyt_ref, *rest):
    pieces, (out_ref, w_ref, sems) = rest[:-3], rest[-3:]
    fetch(pieces, w_ref, sems)
    for e in range(2):
        out_ref[rows_of(e), :] = tn(chunks_of(s_ref, 0, n, dyt_ref, rows_of(e)), w_ref[...])


def near(scalars, dyt, pieces, name):
    width, tok = dyt.shape
    ff, n = pieces[0].shape[1], len(pieces)
    return call(
        functools.partial(near_kernel, n),
        name,
        [SMEM, VMEM] + [HBM] * n,
        VMEM,
        pltpu.VMEM((tok, ff), jnp.float32),
        [pltpu.VMEM((width // 8 * n, ff), jnp.bfloat16), pltpu.SemaphoreType.DMA((n,))],
    )(scalars, in_vmem(dyt), *[in_hbm(a) for a in pieces])


def act_kernel(near_counts, s_ref, dya, dyb, na, nb, ga, gb, gxa, gxb, vda, vdb, *rest):
    pieces, (act_hbm_a, act_hbm_b, v_ref, w_ref, act_ref, sems) = rest[:-6], rest[-6:]
    fetch(pieces, w_ref, sems)
    at = lax.broadcasted_iota(jnp.int32, v_ref.shape, 0)
    value = vda[...] + pltpu.roll(vdb[...], 2, 0)
    copies = []
    depth = w_ref.shape[0]
    for half, (n, dyt, near_ref, gate, gx, act_hbm) in enumerate(
        zip(near_counts, (dya, dyb), (na, nb), (ga, gb), (gxa, gxb), (act_hbm_a, act_hbm_b))
    ):
        below = depth - dyt.shape[0] // 8 * (8 - n)
        w = w_ref[below:, :]
        for e in range(2):
            grad = near_ref[rows_of(e), :] + tn(chunks_of(s_ref, n, 8 - n, dyt, rows_of(e)), w)
            act = (grad * gate[rows_of(e), :].astype(jnp.float32)).astype(jnp.bfloat16)
            k = 2 * half + e
            act_ref[rows_of(k), :] = act
            copies.append(pltpu.make_async_copy(act_ref.at[rows_of(k), :], act_hbm.at[rows_of(e), :], sems.at[8 + k]))
            copies[-1].start()
            value += jnp.where(at == k, jnp.sum(gx[e] * nt(act, act)), 0.0)
    v_ref[...] = value
    for copy in copies:
        copy.wait()


def act_grads(near_counts, scalars, dyt_a, dyt_b, near_a, near_b, gate_a, gate_b, gx_a, gx_b, vd_a, vd_b, pieces):
    width, tok = dyt_a.shape
    ff = near_a.shape[1]
    grads = pltpu.HBM((tok, ff), jnp.bfloat16)
    args = [in_vmem(a) for a in (dyt_a, dyt_b, near_a, near_b, gate_a, gate_b, gx_a, gx_b)]
    return call(
        functools.partial(act_kernel, near_counts),
        "act_grads",
        [SMEM] + [VMEM] * 10 + [HBM] * len(pieces),
        [HBM, HBM, VMEM],
        [grads, grads, jax.ShapeDtypeStruct((8, 128), jnp.float32)],
        [
            pltpu.VMEM((width // 8 * (8 - min(near_counts)), ff), jnp.bfloat16),
            pltpu.VMEM((2 * tok, ff), jnp.bfloat16),
            pltpu.SemaphoreType.DMA((12,)),
        ],
    )(scalars, *args, vd_a, vd_b, *[in_hbm(a) for a in pieces])


def clip_rows(p_ref, q_ref, ra_ref, rb_ref, sa_ref, sb_ref):
    bound = 4.0 * math.sqrt(D * FF)
    sq_norm = jnp.maximum(p_ref[...] + q_ref[...], 0.0)
    clip = bound / jnp.maximum(jnp.sqrt(sq_norm), bound)
    for e in range(2):
        at = rows_of(e)
        sa_ref[at, :] = (ra_ref[at, :].astype(jnp.float32) * clip[e : e + 1, :1]).astype(jnp.bfloat16)
        sb_ref[at, :] = (rb_ref[at, :].astype(jnp.float32) * clip[e + 2 : e + 3, :1]).astype(jnp.bfloat16)


def share_kernel(s_ref, p_ref, q_ref, la_ref, lb_ref, ra_ref, rb_ref, *rest):
    n = s_ref.shape[0]
    outs, (sa_ref, sb_ref) = rest[:n], rest[n:]
    clip_rows(p_ref, q_ref, ra_ref, rb_ref, sa_ref, sb_ref)
    for j, out in enumerate(outs):
        at = chunk(s_ref, j, la_ref)
        out[...] = (nn(la_ref[at, :], sa_ref[...]) + nn(lb_ref[at, :], sb_ref[...])).astype(out.dtype)


def shares(scalars, p, q, lhs_a, lhs_b, rhs_a, rhs_b, dtypes, name):
    tok, ff = rhs_a.shape
    n, rows = scalars.shape[0], lhs_a.shape[0] // 8
    return call(
        share_kernel,
        name,
        [SMEM] + [VMEM] * 6,
        [VMEM] * n,
        [jax.ShapeDtypeStruct((rows, ff), dtype) for dtype in dtypes],
        [pltpu.VMEM((tok, ff), jnp.bfloat16)] * 2,
    )(scalars, p, q, *[in_vmem(a) for a in (lhs_a, lhs_b, rhs_a, rhs_b)])


def all_shares_kernel(dtypes, s_ref, p_ref, q_ref, xa_hbm, xb_hbm, ra_hbm, rb_hbm, *rest):
    outs, (xa_ref, xb_ref, xta_ref, xtb_ref, sa_ref, sb_ref, narrow_ref, wide_ref, sems) = rest[:8], rest[8:]
    copies = [
        pltpu.make_async_copy(src, dst, sems.at[j])
        for j, (src, dst) in enumerate(((xa_hbm, xa_ref), (ra_hbm, sa_ref), (rb_hbm, sb_ref), (xb_hbm, xb_ref)))
    ]
    copies[0].start()
    copies[1].start()
    copies[0].wait()
    copies[2].start()
    copies[3].start()
    xta_ref[...] = xa_ref[...].T
    copies[1].wait()
    copies[2].wait()
    clip_rows(p_ref, q_ref, sa_ref, sb_ref, sa_ref, sb_ref)
    copies[3].wait()
    xtb_ref[...] = xb_ref[...].T
    stores = {jnp.float32: [], jnp.bfloat16: []}
    for j, (dtype, out) in enumerate(zip(dtypes, outs)):
        at = chunk(s_ref, j, xta_ref)
        earlier = stores[dtype]
        held = (wide_ref if dtype == jnp.float32 else narrow_ref).at[len(earlier) % 2]
        if len(earlier) >= 2:
            earlier[-2].wait()
        held[...] = (nn(xta_ref[at, :], sa_ref[...]) + nn(xtb_ref[at, :], sb_ref[...])).astype(dtype)
        earlier.append(pltpu.make_async_copy(held, out, sems.at[4 + j]))
        earlier[-1].start()
    for earlier in stores.values():
        for copy in earlier[-2:]:
            copy.wait()


def all_shares(scalars, p, q, x_a, x_b, rhs_a, rhs_b, dtypes, name):
    tok, ff = rhs_a.shape
    width = x_a.shape[1]
    rows = width // 8
    turned = pltpu.VMEM((width, tok), jnp.bfloat16)
    cols = pltpu.VMEM((tok, ff), jnp.bfloat16)
    return call(
        functools.partial(all_shares_kernel, dtypes),
        name,
        [SMEM, VMEM, VMEM] + [HBM] * 4,
        [HBM] * 8,
        [pltpu.HBM((rows, ff), dtype) for dtype in dtypes],
        [pltpu.VMEM((tok, width), jnp.bfloat16)] * 2
        + [turned, turned, cols, cols]
        + [pltpu.VMEM((2, rows, ff), jnp.bfloat16), pltpu.VMEM((2, rows, ff), jnp.float32)]
        + [pltpu.SemaphoreType.DMA((12,))],
    )(scalars, p, q, *[in_hbm(a) for a in (x_a, x_b, rhs_a, rhs_b)])


def take(hbm_refs, refs, sems):
    copies = [pltpu.make_async_copy(src, dst, sems.at[j]) for j, (src, dst) in enumerate(zip(hbm_refs, refs))]
    for copy in copies:
        copy.start()
    for copy in copies:
        copy.wait()


def join_kernel(staged, *refs):
    ins, (s4_ref, top_ref, bottom_ref), (*held, sems) = refs[:5], refs[5:8], refs[8:]
    f32, bf16 = jnp.float32, jnp.bfloat16
    take(ins if staged else ins[2:], held, sems)
    m4_ref, m3_ref, r2p_ref, r2m_ref, r1_ref = held if staged else list(ins[:2]) + held
    half = top_ref.shape[0]
    s3 = (m3_ref[...] + r1_ref[...].astype(f32)).astype(bf16)
    top_ref[...] = s3[:half]
    bottom_ref[...] = s3[half:]
    s4_ref[...] = (m4_ref[...] + r2p_ref[...].astype(f32) + r2m_ref[...].astype(f32)).astype(bf16)


def join(staged, m4, m3, r2p, r2m, r1, name):
    rows, ff = m4.shape
    bf16 = jnp.bfloat16
    half = jax.ShapeDtypeStruct((rows // 2, ff), bf16)
    arrays = [m4, m3, r2p, r2m, r1]
    held = arrays if staged else arrays[2:]
    return call(
        functools.partial(join_kernel, staged),
        name,
        [HBM if staged else VMEM] * 2 + [HBM] * 3,
        [VMEM] * 3,
        [jax.ShapeDtypeStruct((rows, ff), bf16), half, half],
        [pltpu.VMEM((rows, ff), a.dtype) for a in held] + [pltpu.SemaphoreType.DMA((len(held),))],
    )(*(arrays[: 5 - len(held)] + [in_hbm(a) for a in held]))


def last_hop_kernel(*refs):
    hbm, (sp_ref, sm_ref), (mp_ref, mm_ref, rp_ref, rm_ref, sems) = refs[:4], refs[4:6], refs[6:]
    f32, bf16 = jnp.float32, jnp.bfloat16
    take(hbm, (mp_ref, mm_ref, rp_ref, rm_ref), sems)
    half = rp_ref.shape[0]
    upper, lower = pl.ds(0, half), pl.ds(half, half)
    sp_ref[upper, :] = (mp_ref[upper, :].astype(f32) + rp_ref[...].astype(f32)).astype(bf16)
    sp_ref[lower, :] = mp_ref[lower, :].astype(bf16)
    sm_ref[upper, :] = mm_ref[upper, :].astype(bf16)
    sm_ref[lower, :] = (mm_ref[lower, :].astype(f32) + rm_ref[...].astype(f32)).astype(bf16)


def last_hop(mp, mm, rp, rm, name):
    out = jax.ShapeDtypeStruct(mp.shape, jnp.bfloat16)
    arrays = (mp, mm, rp, rm)
    return call(
        last_hop_kernel,
        name,
        [HBM] * 4,
        [VMEM] * 2,
        [out, out],
        [pltpu.VMEM(a.shape, a.dtype) for a in arrays] + [pltpu.SemaphoreType.DMA((4,))],
    )(*[in_hbm(a) for a in arrays])


def total_kernel(s_ref, *refs):
    (down, up), (kept_d, kept_u, other_ref) = (refs[:4], refs[4:8]), refs[8:]
    half = kept_d.shape[0]
    mine = pl.ds(pl.multiple_of(s_ref[8] * half, 16), half)
    others = pl.ds(pl.multiple_of((1 - s_ref[8]) * half, 16), half)
    for (m, *got), kept, at in ((down, kept_d, 0), (up, kept_u, half)):
        for src, dst in ((mine, kept), (others, other_ref.at[pl.ds(at, half), :])):
            got4, gotp, gotm = [r[src, :].astype(jnp.float32) for r in got]
            dst[...] = (m[src, :] + got4 + gotp + gotm).astype(dst.dtype)


def totals(scalars, down, up):
    rows, ff = down[0].shape
    half = jax.ShapeDtypeStruct((rows // 2, ff), jnp.float32)
    return call(
        total_kernel,
        "totals",
        [SMEM] + [VMEM] * 8,
        [VMEM] * 3,
        [half, half, jax.ShapeDtypeStruct((rows, ff), jnp.bfloat16)],
    )(scalars, *down, *up)


def update_kernel(s_ref, kept_d, kept_u, other_ref, noise_d, noise_u, out_d, out_u):
    half, ff = kept_d.shape
    mine = pl.ds(pl.multiple_of(s_ref[8] * ff, 128), ff)
    others = pl.ds(pl.multiple_of((1 - s_ref[8]) * ff, 128), ff)
    for at, kept, noise, out in ((0, kept_d, noise_d, out_d), (half, kept_u, noise_u, out_u)):
        out[:, mine] = (kept[...] + noise[:, mine]) * (1.0 / (2 * N_DP))
        out[:, others] = (other_ref[pl.ds(at, half), :].astype(jnp.float32) + noise[:, others]) * (1.0 / (2 * N_DP))


def updates(scalars, kept_d, kept_u, other, noise_d, noise_u):
    out = jax.ShapeDtypeStruct(noise_d.shape, jnp.float32)
    return call(update_kernel, "updates", [SMEM] + [VMEM] * 5, [VMEM] * 2, [out, out])(
        scalars, kept_d, kept_u, other, noise_d, noise_u
    )


def after(values, *earlier):
    return lax.optimization_barrier((tuple(values),) + earlier)[0]


def on_device(inputs, up_pre, gate_act, out_grad, down_weight, noise_up, noise_down):
    ff = up_pre.shape[1] // 2
    own_rows = down_weight.shape[0]
    me = lax.axis_index("dp")
    core, x, z = me % 2, (me // 2) % 2, me // 4

    def chip(dz, dx):
        return ((z + dz) % 4) * 2 + ((x + dx) % 2)

    def half_cols(a, which):
        return lax.dynamic_slice(a, (0, which * ff), (a.shape[0], ff))

    def go(a, perm):
        return lax.ppermute(a, "dp", perm)

    near_chips = [chip(0, 0), chip(3, 0), chip(1, 0), chip(0, 1), chip(2, 0)]
    far_chips = [chip(3, 1), chip(1, 1), chip(2, 1)]
    scalars = jnp.stack(near_chips + far_chips + [core]).astype(jnp.int32)

    w_mine = half_cols(down_weight, core)
    w_other = go(half_cols(down_weight, 1 - core), CORE_SWAP)
    own = jnp.where(core == 0, jnp.concatenate([w_mine, w_other]), jnp.concatenate([w_other, w_mine]))
    w_zm = go(own, Z_UP)
    w_zp = go(own, Z_DOWN)
    w_x = go(own, X_SWAP)

    dy_src, x_src = after([out_grad, inputs], own)
    dy_b = go(dy_src, CORE_SWAP)
    x_b = go(x_src, CORE_SWAP)
    x_own, dy_own = after([inputs, out_grad], own)
    dyt_a, gx_a, gate_a, hid_a, vd_a, gu_send = prep_own(scalars, x_own, dy_own, gate_act, up_pre, ff)

    x_b, dy_b = after([x_b, dy_b], vd_a)
    dyt_b, gx_b, gdy_b = prep_other(x_b, dy_b)

    w_zm, w_zp, w_x, gu_send = after([w_zm, w_zp, w_x, gu_send], dyt_b)
    up_half, down_half = halves(w_zm, w_zp)
    w_z2_top = go(up_half, Z_UP)
    w_z2_bot = go(down_half, Z_DOWN)
    gu_b = go(gu_send, CORE_SWAP)
    w_x = after([w_x], up_half)[0]
    w_zm_x = go(w_x, Z_UP)
    w_zp_x = go(w_x, Z_DOWN)
    near_a = near(scalars, after([dyt_a], up_half)[0], [own, w_zm, w_zp, w_x], "near_own")
    w_z2_top, w_z2_bot = after([w_z2_top, w_z2_bot], near_a)
    w_z2 = jnp.concatenate([w_z2_top, w_z2_bot])
    w_z2_x = go(w_z2, X_SWAP)
    hid_b, vd_b = hidden_other(after([gu_b], w_z2)[0], gdy_b)
    near_b = near(scalars, after([dyt_b], hid_b)[0], [own, w_zm, w_zp, w_x, w_z2], "near_other")
    w_zm_x, w_zp_x, w_z2_x = after([w_zm_x, w_zp_x, w_z2_x], near_b, vd_b)
    far_pieces = [w_z2, w_zm_x, w_zp_x, w_z2_x]
    act_a, act_b, part = act_grads(
        (4, 5), scalars, dyt_a, dyt_b, near_a, near_b, gate_a, gu_b, gx_a, gx_b, vd_a, vd_b, far_pieces
    )

    got = go(part, CORE_SWAP)
    part = part + jnp.concatenate([got[2:4], got[0:2], got[4:]])
    for swap in TENSOR_SWAPS[:2]:
        part = part + lax.ppermute(part, "tensor", swap)
    rest = lax.ppermute(part, "tensor", TENSOR_SWAPS[2])

    early_chips = [chip(1, 1), chip(3, 1), chip(2, 1)]
    late_chips = [chip(0, 1), chip(2, 0), chip(1, 0), chip(3, 0), chip(0, 0)]
    early = jnp.stack(early_chips).astype(jnp.int32)
    late = jnp.stack(late_chips).astype(jnp.int32)
    every = jnp.concatenate([early, late])

    f32, bf16 = jnp.float32, jnp.bfloat16
    kinds = [f32, f32, bf16, bf16, f32]
    down_args = (part, rest, dyt_a, dyt_b, hid_a, hid_b)
    down_p, down_m, down_x = shares(early, *down_args, [bf16] * 3, "down_first")
    d2p, d2m, d1 = go(down_p, Z_UP), go(down_m, Z_DOWN), go(down_x, X_SWAP)
    act_a, act_b = after([act_a, act_b], down_x)
    up_p, up_m, up_x, up4, up3, up5p, up5m, up_own = all_shares(
        every, part, rest, inputs, x_b, act_a, act_b, [bf16] * 3 + kinds, "up_all"
    )
    d2p, d2m, d1 = after([d2p, d2m, d1], up_x)
    u2p, u2m, u1 = go(up_p, Z_UP), go(up_m, Z_DOWN), go(up_x, X_SWAP)
    late2 = after([late], d2p, d2m)[0]
    down4, down3, down5p, down5m, down_own = shares(late2, *down_args, kinds, "down_later")
    s4d, s3dt, s3db = join(False, down4, down3, d2p, d2m, d1, "down_join")
    d3p, d3m, d4 = go(s3dt, Z_UP), go(s3db, Z_DOWN), go(s4d, X_SWAP)
    u2p, u2m, u1 = after([u2p, u2m, u1], s3dt)
    s4u, s3ut, s3ub = join(True, up4, up3, u2p, u2m, u1, "up_join")
    u3p, u3m, u4 = go(s3ut, Z_UP), go(s3ub, Z_DOWN), go(s4u, X_SWAP)
    d3p, d3m, d4 = after([d3p, d3m, d4], s3ut)
    d3p, d3m = after([d3p, d3m], d4)
    s5dp, s5dm = last_hop(down5p, down5m, d3p, d3m, "down_last")
    d5p, d5m = go(s5dp, Z_UP), go(s5dm, Z_DOWN)
    u3p, u3m = after([u3p, u3m], s5dp)
    s5up, s5um = last_hop(up5p, up5m, u3p, u3m, "up_last")
    u5p, u5m = go(s5up, Z_UP), go(s5um, Z_DOWN)

    d5p, d5m, u4 = after([d5p, d5m, u4], s5up)
    kept_d, kept_u, other = totals(scalars, (down_own, d4, d5p, d5m), (up_own, u4, u5p, u5m))
    other = go(other, CORE_SWAP)
    down_update, up_update = updates(scalars, kept_d, kept_u, other, noise_down, noise_up)
    return (up_update, down_update)


def solution(mesh):
    in_specs = (
        P("dp", None),
        P("dp", "tensor"),
        P("dp", "tensor"),
        P("dp", None),
        P("dp", "tensor"),
        P("dp", "tensor"),
        P("dp", "tensor"),
    )
    out_specs = (P("dp", "tensor"), P("dp", "tensor"))
    return jax.shard_map(
        on_device, mesh=mesh, in_specs=in_specs, out_specs=out_specs, check_vma=False
    )
```

```python
import functools
import math

import jax
import jax.numpy as jnp
from jax import lax
from jax.experimental import pallas as pl
from jax.experimental.pallas import tpu as pltpu
from jax.sharding import PartitionSpec as P

D = 2304
FF = 18432
SEQ = 384
N_DP = 16
N_TENSOR = 8
COST = pl.CostEstimate(flops=1000, bytes_accessed=1000, transcendentals=0)

Z_UP = [(i, (i + 4) % 16) for i in range(16)]
Z_DOWN = [(i, (i + 12) % 16) for i in range(16)]
X_SWAP = [(i, i ^ 2) for i in range(16)]
CORE_SWAP = [(i, i ^ 1) for i in range(16)]
TENSOR_SWAPS = [[(t, t ^ k) for t in range(8)] for k in (4, 1, 3)]


VMEM = pl.BlockSpec(memory_space=pltpu.VMEM)
SMEM = pl.BlockSpec(memory_space=pltpu.SMEM)
HBM = pl.BlockSpec(memory_space=pl.ANY)


def in_vmem(a):
    return pltpu.with_memory_space_constraint(a, pltpu.VMEM)


def in_hbm(a):
    return pltpu.with_memory_space_constraint(a, pltpu.HBM)


def nt(a, b):
    return lax.dot_general(a, b, (((1,), (1,)), ((), ())), preferred_element_type=jnp.float32)


def nn(a, b):
    return lax.dot_general(a, b, (((1,), (0,)), ((), ())), preferred_element_type=jnp.float32)


def tn(a, b):
    return lax.dot_general(a, b, (((0,), (0,)), ((), ())), preferred_element_type=jnp.float32)


def call(kernel, name, in_specs, out_specs, out_shape, scratch=(), mib=21):
    return pl.pallas_call(
        kernel,
        in_specs=in_specs,
        out_specs=out_specs,
        out_shape=out_shape,
        scratch_shapes=list(scratch),
        compiler_params=pltpu.CompilerParams(vmem_limit_bytes=mib << 20),
        cost_estimate=COST,
        name=name,
    )


def rows_of(e):
    return pl.ds(e * SEQ, SEQ)


def chunk(s_ref, j, ref):
    rows = ref.shape[0] // 8
    return pl.ds(pl.multiple_of(s_ref[j] * rows, 32), rows)


def turn(x_ref, dy_ref, xt_ref, dyt_ref, gx_ref, gdy_ref, arrivals):
    for e in range(2):
        arrivals[2 * e].wait()
        x = x_ref[rows_of(e), :]
        xt_ref[:, rows_of(e)] = x.T
        gx_ref[e] = nt(x, x)
        arrivals[2 * e + 1].wait()
        dy = dy_ref[rows_of(e), :]
        dyt_ref[:, rows_of(e)] = dy.T
        gdy_ref[e] = nt(dy, dy)


def token_copies(x_hbm, dy_hbm, x_ref, dy_ref, sems):
    pairs = []
    for e in range(2):
        for src, dst in ((x_hbm, x_ref), (dy_hbm, dy_ref)):
            pairs.append((src.at[rows_of(e), :], dst.at[rows_of(e), :]))
    return [pltpu.make_async_copy(src, dst, sems.at[j]) for j, (src, dst) in enumerate(pairs)]


def hidden_norm(gate_ref, up_ref, gdy_ref, hid_ref, vd_ref):
    at = lax.broadcasted_iota(jnp.int32, vd_ref.shape, 0)
    value = jnp.zeros(vd_ref.shape, jnp.float32)
    for e in range(2):
        gate, up = gate_ref[rows_of(e), :].astype(jnp.float32), up_ref[rows_of(e), :].astype(jnp.float32)
        hid = (gate * up).astype(jnp.bfloat16)
        hid_ref[rows_of(e), :] = hid
        value += jnp.where(at == e, jnp.sum(gdy_ref[e] * nt(hid, hid)), 0.0)
    vd_ref[...] = value


def own_kernel(
    s_ref, x_hbm, dy_hbm, gate_hbm, up_hbm, xt_hbm, dyt_ref, gx_hbm, gate_ref, hid_ref, vd_ref, sent_ref,
    x_ref, dy_ref, xt_ref, up_ref, gx_ref, gdy_ref, sems,
):
    tok, ff = hid_ref.shape
    tokens = token_copies(x_hbm, dy_hbm, x_ref, dy_ref, sems)
    mine = pl.ds(pl.multiple_of(s_ref[8] * ff, 128), ff)
    other = pl.ds(pl.multiple_of((1 - s_ref[8]) * ff, 128), ff)
    pairs = [
        (gate_hbm.at[:, mine], gate_ref),
        (up_hbm.at[:, mine], up_ref),
        (gate_hbm.at[:, other], sent_ref.at[pl.ds(0, tok), :]),
        (up_hbm.at[:, other], sent_ref.at[pl.ds(tok, tok), :]),
    ]
    columns = [pltpu.make_async_copy(src, dst, sems.at[4 + j]) for j, (src, dst) in enumerate(pairs)]
    for copy in tokens + columns:
        copy.start()
    turn(x_ref, dy_ref, xt_ref, dyt_ref, gx_ref, gdy_ref, tokens)
    keep = [pltpu.make_async_copy(gx_ref, gx_hbm, sems.at[8]), pltpu.make_async_copy(xt_ref, xt_hbm, sems.at[9])]
    for copy in keep:
        copy.start()
    columns[0].wait()
    columns[1].wait()
    hidden_norm(gate_ref, up_ref, gdy_ref, hid_ref, vd_ref)
    for copy in columns[2:] + keep:
        copy.wait()


def prep_own(scalars, x, dy, gate, up, ff):
    tok, width = x.shape
    bf16, f32 = jnp.bfloat16, jnp.float32
    cols = pltpu.VMEM((tok, ff), bf16)
    gram = (2, SEQ, SEQ)
    return call(
        own_kernel,
        "prep_own",
        [SMEM] + [HBM] * 4,
        [HBM, VMEM, HBM] + [VMEM] * 4,
        [
            pltpu.HBM((width, tok), bf16),
            pltpu.VMEM((width, tok), bf16),
            pltpu.HBM(gram, f32),
            cols,
            cols,
            jax.ShapeDtypeStruct((8, 128), f32),
            pltpu.VMEM((2 * tok, ff), bf16),
        ],
        [pltpu.VMEM((tok, width), bf16)] * 2
        + [pltpu.VMEM((width, tok), bf16), cols, pltpu.VMEM(gram, f32), pltpu.VMEM(gram, f32)]
        + [pltpu.SemaphoreType.DMA((10,))],
    )(scalars, *[in_hbm(a) for a in (x, dy, gate, up)])


def other_kernel(x_hbm, dy_hbm, xt_hbm, dyt_ref, gx_hbm, gdy_ref, x_ref, dy_ref, xt_ref, gx_ref, sems):
    tokens = token_copies(x_hbm, dy_hbm, x_ref, dy_ref, sems)
    for copy in tokens:
        copy.start()
    turn(x_ref, dy_ref, xt_ref, dyt_ref, gx_ref, gdy_ref, tokens)
    keep = [pltpu.make_async_copy(gx_ref, gx_hbm, sems.at[4]), pltpu.make_async_copy(xt_ref, xt_hbm, sems.at[5])]
    for copy in keep:
        copy.start()
    for copy in keep:
        copy.wait()


def prep_other(x, dy):
    tok, width = x.shape
    bf16, f32 = jnp.bfloat16, jnp.float32
    gram = (2, SEQ, SEQ)
    return call(
        other_kernel,
        "prep_other",
        [HBM] * 2,
        [HBM, VMEM, HBM, VMEM],
        [pltpu.HBM((width, tok), bf16), pltpu.VMEM((width, tok), bf16), pltpu.HBM(gram, f32), pltpu.VMEM(gram, f32)],
        [pltpu.VMEM((tok, width), bf16)] * 2
        + [pltpu.VMEM((width, tok), bf16), pltpu.VMEM(gram, f32), pltpu.SemaphoreType.DMA((6,))],
    )(in_hbm(x), in_hbm(dy))


def hidden_kernel(gu_ref, gdy_ref, hid_ref, vd_ref):
    tok = hid_ref.shape[0]
    hidden_norm(gu_ref.at[pl.ds(0, tok), :], gu_ref.at[pl.ds(tok, tok), :], gdy_ref, hid_ref, vd_ref)


def hidden_other(gu, gdy):
    tok, ff = gu.shape[0] // 2, gu.shape[1]
    return call(
        hidden_kernel,
        "hidden_other",
        [VMEM] * 2,
        [VMEM] * 2,
        [pltpu.VMEM((tok, ff), jnp.bfloat16), jax.ShapeDtypeStruct((8, 128), jnp.float32)],
    )(in_vmem(gu), in_vmem(gdy))


def halves_kernel(a_ref, b_ref, top_ref, bottom_ref, sems):
    half = top_ref.shape[0]
    copies = [
        pltpu.make_async_copy(a_ref.at[pl.ds(0, half), :], top_ref, sems.at[0]),
        pltpu.make_async_copy(b_ref.at[pl.ds(half, half), :], bottom_ref, sems.at[1]),
    ]
    for copy in copies:
        copy.start()
    for copy in copies:
        copy.wait()


def halves(a, b):
    half = pltpu.VMEM((a.shape[0] // 2, a.shape[1]), a.dtype)
    return call(halves_kernel, "halves", [HBM] * 2, [VMEM] * 2, [half, half], [pltpu.SemaphoreType.DMA((2,))])(
        in_hbm(a), in_hbm(b)
    )


def fetch(pieces, w_ref, sems):
    copies, at = [], 0
    for j, piece in enumerate(pieces):
        n = piece.shape[0]
        copies.append(pltpu.make_async_copy(piece, w_ref.at[pl.ds(at, n), :], sems.at[j]))
        at += n
    for copy in copies:
        copy.start()
    for copy in copies:
        copy.wait()


def chunks_of(s_ref, first, n, ref, columns):
    return jnp.concatenate([ref[chunk(s_ref, j, ref), columns] for j in range(first, first + n)])


def near_kernel(n, s_ref, dyt_ref, *rest):
    pieces, (out_ref, w_ref, sems) = rest[:-3], rest[-3:]
    fetch(pieces, w_ref, sems)
    for e in range(2):
        out_ref[rows_of(e), :] = tn(chunks_of(s_ref, 0, n, dyt_ref, rows_of(e)), w_ref[...])


def near(scalars, dyt, pieces, name):
    width, tok = dyt.shape
    ff, n = pieces[0].shape[1], len(pieces)
    return call(
        functools.partial(near_kernel, n),
        name,
        [SMEM, VMEM] + [HBM] * n,
        VMEM,
        pltpu.VMEM((tok, ff), jnp.float32),
        [pltpu.VMEM((width // 8 * n, ff), jnp.bfloat16), pltpu.SemaphoreType.DMA((n,))],
    )(scalars, in_vmem(dyt), *[in_hbm(a) for a in pieces])


def act_kernel(near_counts, s_ref, dya, dyb, na, nb, ga, gb, gxa_hbm, gxb_hbm, vda, vdb, *rest):
    pieces, (act_hbm_a, act_hbm_b, v_ref, w_ref, act_ref, gxa, gxb, sems) = rest[:-8], rest[-8:]
    grams = [pltpu.make_async_copy(gxa_hbm, gxa, sems.at[12]), pltpu.make_async_copy(gxb_hbm, gxb, sems.at[13])]
    for copy in grams:
        copy.start()
    fetch(pieces, w_ref, sems)
    at = lax.broadcasted_iota(jnp.int32, v_ref.shape, 0)
    value = vda[...] + pltpu.roll(vdb[...], 2, 0)
    copies = []
    depth = w_ref.shape[0]
    for half, (n, dyt, near_ref, gate, gx, act_hbm) in enumerate(
        zip(near_counts, (dya, dyb), (na, nb), (ga, gb), (gxa, gxb), (act_hbm_a, act_hbm_b))
    ):
        below = depth - dyt.shape[0] // 8 * (8 - n)
        grams[half].wait()
        w = w_ref[below:, :]
        for e in range(2):
            grad = near_ref[rows_of(e), :] + tn(chunks_of(s_ref, n, 8 - n, dyt, rows_of(e)), w)
            act = (grad * gate[rows_of(e), :].astype(jnp.float32)).astype(jnp.bfloat16)
            k = 2 * half + e
            act_ref[rows_of(k), :] = act
            copies.append(pltpu.make_async_copy(act_ref.at[rows_of(k), :], act_hbm.at[rows_of(e), :], sems.at[8 + k]))
            copies[-1].start()
            value += jnp.where(at == k, jnp.sum(gx[e] * nt(act, act)), 0.0)
    v_ref[...] = value
    for copy in copies:
        copy.wait()


def act_grads(near_counts, scalars, dyt_a, dyt_b, near_a, near_b, gate_a, gate_b, gx_a, gx_b, vd_a, vd_b, pieces):
    width, tok = dyt_a.shape
    ff = near_a.shape[1]
    grads = pltpu.HBM((tok, ff), jnp.bfloat16)
    args = [in_vmem(a) for a in (dyt_a, dyt_b, near_a, near_b, gate_a, gate_b)] + [in_hbm(gx_a), in_hbm(gx_b)]
    return call(
        functools.partial(act_kernel, near_counts),
        "act_grads",
        [SMEM] + [VMEM] * 6 + [HBM] * 2 + [VMEM] * 2 + [HBM] * len(pieces),
        [HBM, HBM, VMEM],
        [grads, grads, jax.ShapeDtypeStruct((8, 128), jnp.float32)],
        [
            pltpu.VMEM((width // 8 * (8 - min(near_counts)), ff), jnp.bfloat16),
            pltpu.VMEM((2 * tok, ff), jnp.bfloat16),
            pltpu.VMEM(gx_a.shape, gx_a.dtype),
            pltpu.VMEM(gx_b.shape, gx_b.dtype),
            pltpu.SemaphoreType.DMA((14,)),
        ],
    )(scalars, *args, vd_a, vd_b, *pieces)


def clips(p_ref, q_ref):
    bound = 4.0 * math.sqrt(D * FF)
    sq_norm = jnp.maximum(p_ref[...] + q_ref[...], 0.0)
    return bound / jnp.maximum(jnp.sqrt(sq_norm), bound)


def clip_rows(clip, first, src_ref, dst_ref):
    for e in range(2):
        at = rows_of(e)
        scale = clip[first + e : first + e + 1, :1]
        dst_ref[at, :] = (src_ref[at, :].astype(jnp.float32) * scale).astype(jnp.bfloat16)


def pair_copies(s_ref, n, a_hbm, b_hbm, dst_ref, sems, first):
    rows = dst_ref.shape[1]
    copies = []
    for k, src in enumerate((a_hbm, b_hbm)):
        for j in range(n):
            at = pl.ds(pl.multiple_of(s_ref[j] * rows, 32), rows)
            copies.append(pltpu.make_async_copy(src.at[at, :], dst_ref.at[k * n + j], sems.at[first + k * n + j]))
    return copies


def down_first_kernel(s_ref, p_ref, q_ref, la_ref, lb_ref, ra_ref, rb_ref, *rest):
    outs, (sa_ref, sb_ref, o_ref, sems) = rest[:3], rest[3:]
    clip = clips(p_ref, q_ref)
    clip_rows(clip, 0, ra_ref, sa_ref)
    clip_rows(clip, 2, rb_ref, sb_ref)
    copies = []
    for j, out in enumerate(outs):
        at = chunk(s_ref, j, la_ref)
        o_ref[j] = (nn(la_ref[at, :], sa_ref[...]) + nn(lb_ref[at, :], sb_ref[...])).astype(o_ref.dtype)
        copies.append(pltpu.make_async_copy(o_ref.at[j], out, sems.at[j]))
        copies[-1].start()
    for copy in copies:
        copy.wait()


def down_first(scalars, p, q, dyt_a, dyt_b, hid_a, hid_b):
    tok, ff = hid_a.shape
    rows = dyt_a.shape[0] // 8
    bf16 = jnp.bfloat16
    cols = pltpu.VMEM((tok, ff), bf16)
    return call(
        down_first_kernel,
        "down_first",
        [SMEM] + [VMEM] * 6,
        [HBM] * 3,
        [pltpu.HBM((rows, ff), bf16)] * 3,
        [cols, cols, pltpu.VMEM((3, rows, ff), bf16), pltpu.SemaphoreType.DMA((3,))],
    )(scalars, p, q, *[in_vmem(a) for a in (dyt_a, dyt_b, hid_a, hid_b)])


def up_all_kernel(
    dtypes, e_ref, s_ref, p_ref, q_ref, acta_hbm, actb_hbm, xta_hbm, xtb_hbm, ha_hbm, hb_hbm, dya_hbm, dyb_hbm, *rest
):
    outs, (ha_ref, hb_ref, dy_ref, x_ref, l_ref, sa_ref, sb_ref, narrow_ref, wide_ref, sems) = rest[:8], rest[8:]
    first = [
        pltpu.make_async_copy(acta_hbm, sa_ref, sems.at[30]),
        pltpu.make_async_copy(actb_hbm, sb_ref, sems.at[31]),
    ] + pair_copies(e_ref, 3, xta_hbm, xtb_hbm, x_ref, sems, 32)
    loads = pair_copies(s_ref, 5, xta_hbm, xtb_hbm, l_ref, sems, 0)
    for copy in first:
        copy.start()
    ahead = [
        pltpu.make_async_copy(ha_hbm, ha_ref, sems.at[10]),
        pltpu.make_async_copy(hb_hbm, hb_ref, sems.at[11]),
    ] + pair_copies(s_ref, 5, dya_hbm, dyb_hbm, dy_ref, sems, 12)
    clip = clips(p_ref, q_ref)
    first[0].wait()
    clip_rows(clip, 0, sa_ref, sa_ref)
    first[1].wait()
    clip_rows(clip, 2, sb_ref, sb_ref)
    for copy in first[2:]:
        copy.wait()
    for copy in loads:
        copy.start()
    stores = {jnp.float32: [], jnp.bfloat16: []}
    for j, (dtype, out) in enumerate(zip(dtypes, outs)):
        if j == 3:
            for copy in loads:
                copy.wait()
            for copy in ahead:
                copy.start()
        a, b = (x_ref[j], x_ref[3 + j]) if j < 3 else (l_ref[j - 3], l_ref[j + 2])
        earlier = stores[dtype]
        held = (wide_ref if dtype == jnp.float32 else narrow_ref).at[len(earlier)]
        held[...] = (nn(a, sa_ref[...]) + nn(b, sb_ref[...])).astype(dtype)
        earlier.append(pltpu.make_async_copy(held, out, sems.at[22 + j]))
        earlier[-1].start()
    for copy in ahead + stores[jnp.float32] + stores[jnp.bfloat16]:
        copy.wait()


def up_all(early, late_chunks, p, q, act_a, act_b, xt_a, xt_b, hid_a, hid_b, dyt_a, dyt_b, dtypes):
    tok, ff = act_a.shape
    rows = xt_a.shape[0] // 8
    bf16 = jnp.bfloat16
    cols = pltpu.VMEM((tok, ff), bf16)
    late = pltpu.VMEM((10, rows, tok), bf16)
    wide = sum(dtype == jnp.float32 for dtype in dtypes)
    return call(
        functools.partial(up_all_kernel, dtypes),
        "up_all",
        [SMEM] * 2 + [VMEM] * 2 + [HBM] * 8,
        [HBM] * 8 + [VMEM] * 3,
        [pltpu.HBM((rows, ff), dtype) for dtype in dtypes] + [cols, cols, late],
        [pltpu.VMEM((6, rows, tok), bf16), late, cols, cols, pltpu.VMEM((8 - wide, rows, ff), bf16), pltpu.VMEM((wide, rows, ff), jnp.float32)]
        + [pltpu.SemaphoreType.DMA((38,))],
        26,
    )(early, late_chunks, p, q, *[in_hbm(a) for a in (act_a, act_b, xt_a, xt_b, hid_a, hid_b, dyt_a, dyt_b)])


def down_later_kernel(p_ref, q_ref, ha_ref, hb_ref, dy_ref, *rest):
    got_hbm, outs, got_refs, (sa_ref, sb_ref, sems) = rest[:3], rest[3:9], rest[9:12], rest[12:]
    got = [pltpu.make_async_copy(src, dst, sems.at[j]) for j, (src, dst) in enumerate(zip(got_hbm, got_refs))]
    for copy in got:
        copy.start()
    clip = clips(p_ref, q_ref)
    clip_rows(clip, 0, ha_ref, sa_ref)
    clip_rows(clip, 2, hb_ref, sb_ref)

    def share(j):
        return nn(dy_ref[j], sa_ref[...]) + nn(dy_ref[5 + j], sb_ref[...])

    for j, out in enumerate(outs[3:]):
        out[...] = share(2 + j).astype(out.dtype)
    for copy in got:
        copy.wait()
    tree_add(share(0), share(1), *got_refs, *outs[:3])


def down_later(p, q, hid_a, hid_b, dy_late, got, dtypes):
    tok, ff = hid_a.shape
    rows = dy_late.shape[1]
    bf16 = jnp.bfloat16
    half = jax.ShapeDtypeStruct((rows // 2, ff), bf16)
    cols = pltpu.VMEM((tok, ff), bf16)
    return call(
        down_later_kernel,
        "down_later",
        [VMEM] * 5 + [HBM] * 3,
        [VMEM] * 6,
        [jax.ShapeDtypeStruct((rows, ff), bf16), half, half]
        + [jax.ShapeDtypeStruct((rows, ff), dtype) for dtype in dtypes],
        [pltpu.VMEM((rows, ff), bf16)] * 3 + [cols, cols, pltpu.SemaphoreType.DMA((3,))],
    )(p, q, *[in_vmem(a) for a in (hid_a, hid_b, dy_late)], *got)


def tree_add(m4, m3, r1_ref, r2p_ref, r2m_ref, s4_ref, top_ref, bottom_ref):
    f32, bf16 = jnp.float32, jnp.bfloat16
    half = top_ref.shape[0]
    s3 = (m3 + r1_ref[...].astype(f32)).astype(bf16)
    top_ref[...] = s3[:half]
    bottom_ref[...] = s3[half:]
    s4_ref[...] = (m4 + r2p_ref[...].astype(f32) + r2m_ref[...].astype(f32)).astype(bf16)


def take(hbm_refs, refs, sems):
    copies = [pltpu.make_async_copy(src, dst, sems.at[j]) for j, (src, dst) in enumerate(zip(hbm_refs, refs))]
    for copy in copies:
        copy.start()
    for copy in copies:
        copy.wait()


def join_kernel(*refs):
    ins, outs, (*held, sems) = refs[:5], refs[5:8], refs[8:]
    take(ins, held, sems)
    m4_ref, m3_ref, *got = held
    tree_add(m4_ref[...], m3_ref[...], *got, *outs)


def join(m4, m3, r1, r2p, r2m, name):
    rows, ff = m4.shape
    bf16 = jnp.bfloat16
    half = jax.ShapeDtypeStruct((rows // 2, ff), bf16)
    arrays = [in_hbm(m4), in_hbm(m3), r1, r2p, r2m]
    return call(
        join_kernel,
        name,
        [HBM] * 5,
        [VMEM] * 3,
        [jax.ShapeDtypeStruct((rows, ff), bf16), half, half],
        [pltpu.VMEM((rows, ff), a.dtype) for a in arrays] + [pltpu.SemaphoreType.DMA((5,))],
    )(*arrays)


def last_hop_kernel(*refs):
    hbm, (sp_ref, sm_ref), (mp_ref, mm_ref, rp_ref, rm_ref, sems) = refs[:4], refs[4:6], refs[6:]
    f32, bf16 = jnp.float32, jnp.bfloat16
    take(hbm, (mp_ref, mm_ref, rp_ref, rm_ref), sems)
    half = rp_ref.shape[0]
    upper, lower = pl.ds(0, half), pl.ds(half, half)
    sp_ref[upper, :] = (mp_ref[upper, :].astype(f32) + rp_ref[...].astype(f32)).astype(bf16)
    sp_ref[lower, :] = mp_ref[lower, :].astype(bf16)
    sm_ref[upper, :] = mm_ref[upper, :].astype(bf16)
    sm_ref[lower, :] = (mm_ref[lower, :].astype(f32) + rm_ref[...].astype(f32)).astype(bf16)


def last_hop(mp, mm, rp, rm, name):
    out = jax.ShapeDtypeStruct(mp.shape, jnp.bfloat16)
    arrays = (mp, mm, rp, rm)
    return call(
        last_hop_kernel,
        name,
        [HBM] * 4,
        [VMEM] * 2,
        [out, out],
        [pltpu.VMEM(a.shape, a.dtype) for a in arrays] + [pltpu.SemaphoreType.DMA((4,))],
    )(*arrays)


def total_kernel(s_ref, *refs):
    (down, up), (kept_d, kept_u, other_ref) = (refs[:4], refs[4:8]), refs[8:]
    half = kept_d.shape[0]
    mine = pl.ds(pl.multiple_of(s_ref[8] * half, 16), half)
    others = pl.ds(pl.multiple_of((1 - s_ref[8]) * half, 16), half)
    for (m, *got), kept, at in ((down, kept_d, 0), (up, kept_u, half)):
        for src, dst in ((mine, kept), (others, other_ref.at[pl.ds(at, half), :])):
            got4, gotp, gotm = [r[src, :].astype(jnp.float32) for r in got]
            dst[...] = (m[src, :] + got4 + gotp + gotm).astype(dst.dtype)


def totals(scalars, down, up):
    rows, ff = down[0].shape
    half = jax.ShapeDtypeStruct((rows // 2, ff), jnp.float32)
    return call(
        total_kernel,
        "totals",
        [SMEM] + [VMEM] * 8,
        [VMEM] * 3,
        [half, half, jax.ShapeDtypeStruct((rows, ff), jnp.bfloat16)],
    )(scalars, *down, *up)


def update_kernel(s_ref, kept_d, kept_u, other_ref, noise_d, noise_u, out_d, out_u):
    half, ff = kept_d.shape
    mine = pl.ds(pl.multiple_of(s_ref[8] * ff, 128), ff)
    others = pl.ds(pl.multiple_of((1 - s_ref[8]) * ff, 128), ff)
    for at, kept, noise, out in ((0, kept_d, noise_d, out_d), (half, kept_u, noise_u, out_u)):
        out[:, mine] = (kept[...] + noise[:, mine]) * (1.0 / (2 * N_DP))
        out[:, others] = (other_ref[pl.ds(at, half), :].astype(jnp.float32) + noise[:, others]) * (1.0 / (2 * N_DP))


def updates(scalars, kept_d, kept_u, other, noise_d, noise_u):
    out = jax.ShapeDtypeStruct(noise_d.shape, jnp.float32)
    return call(update_kernel, "updates", [SMEM] + [VMEM] * 5, [VMEM] * 2, [out, out])(
        scalars, kept_d, kept_u, other, noise_d, noise_u
    )


def after(values, *earlier):
    return lax.optimization_barrier((tuple(values),) + earlier)[0]


def on_device(inputs, up_pre, gate_act, out_grad, down_weight, noise_up, noise_down):
    ff = up_pre.shape[1] // 2
    own_rows = down_weight.shape[0]
    me = lax.axis_index("dp")
    core, x, z = me % 2, (me // 2) % 2, me // 4

    def chip(dz, dx):
        return ((z + dz) % 4) * 2 + ((x + dx) % 2)

    def half_cols(a, which):
        return lax.dynamic_slice(a, (0, which * ff), (a.shape[0], ff))

    def go(a, perm):
        return lax.ppermute(a, "dp", perm)

    near_chips = [chip(0, 0), chip(3, 0), chip(1, 0), chip(0, 1), chip(2, 0)]
    far_chips = [chip(3, 1), chip(1, 1), chip(2, 1)]
    scalars = jnp.stack(near_chips + far_chips + [core]).astype(jnp.int32)

    w_mine = half_cols(down_weight, core)
    w_other = go(half_cols(down_weight, 1 - core), CORE_SWAP)
    own = jnp.where(core == 0, jnp.concatenate([w_mine, w_other]), jnp.concatenate([w_other, w_mine]))
    w_x = go(own, X_SWAP)
    w_zp = go(own, Z_DOWN)
    w_zm = go(own, Z_UP)

    dy_src, x_src = after([out_grad, inputs], own)
    dy_b = go(dy_src, CORE_SWAP)
    x_b = go(x_src, CORE_SWAP)
    x_own, dy_own = after([inputs, out_grad], own)
    xt_a, dyt_a, gx_a, gate_a, hid_a, vd_a, gu_send = prep_own(scalars, x_own, dy_own, gate_act, up_pre, ff)

    x_b, dy_b = after([x_b, dy_b], vd_a)
    xt_b, dyt_b, gx_b, gdy_b = prep_other(x_b, dy_b)

    w_x, w_zp, w_zm, gu_send = after([w_x, w_zp, w_zm, gu_send], dyt_b)
    up_half, down_half = halves(w_zm, w_zp)
    w_z2_top = go(up_half, Z_UP)
    w_z2_bot = go(down_half, Z_DOWN)
    gu_b = go(gu_send, CORE_SWAP)
    w_x = after([w_x], up_half)[0]
    w_zm_x = go(w_x, Z_UP)
    w_zp_x = go(w_x, Z_DOWN)
    near_a = near(scalars, after([dyt_a], up_half)[0], [own, w_zm, w_zp, w_x], "near_own")
    w_z2_top, w_z2_bot = after([w_z2_top, w_z2_bot], near_a)
    w_z2 = jnp.concatenate([w_z2_top, w_z2_bot])
    w_z2_x = go(w_z2, X_SWAP)
    hid_b, vd_b = hidden_other(after([gu_b], w_z2)[0], gdy_b)
    near_b = near(scalars, after([dyt_b], hid_b)[0], [own, w_zm, w_zp, w_x, w_z2], "near_other")
    w_zm_x, w_zp_x, w_z2_x = after([w_zm_x, w_zp_x, w_z2_x], near_b, vd_b)
    far_pieces = [w_z2, w_zm_x, w_zp_x, w_z2_x]
    act_a, act_b, part = act_grads(
        (4, 5), scalars, dyt_a, dyt_b, near_a, near_b, gate_a, gu_b, gx_a, gx_b, vd_a, vd_b, far_pieces
    )

    got = go(part, CORE_SWAP)
    part = part + jnp.concatenate([got[2:4], got[0:2], got[4:]])
    for swap in TENSOR_SWAPS[:2]:
        part = part + lax.ppermute(part, "tensor", swap)
    rest = lax.ppermute(part, "tensor", TENSOR_SWAPS[2])

    early_chips = [chip(1, 1), chip(3, 1), chip(2, 1)]
    late_chips = [chip(0, 1), chip(2, 0), chip(1, 0), chip(3, 0), chip(0, 0)]
    early = jnp.stack(early_chips).astype(jnp.int32)
    late = jnp.stack(late_chips).astype(jnp.int32)

    f32, bf16 = jnp.float32, jnp.bfloat16
    down_p, down_m, down_x = down_first(early, part, rest, dyt_a, dyt_b, hid_a, hid_b)
    d1, d2p, d2m = go(down_x, X_SWAP), go(down_p, Z_UP), go(down_m, Z_DOWN)
    up_p, up_m, up_x, up4, up3, up5p, up5m, up_own, hid_a, hid_b, dy_late = up_all(
        early, late, part, rest, *after([act_a, act_b], down_x), xt_a, xt_b, hid_a, hid_b, dyt_a, dyt_b,
        [bf16] * 3 + [f32, f32, bf16, bf16, f32],
    )
    d1, d2p, d2m = after([d1, d2p, d2m], up_x)
    u1, u2p, u2m = go(up_x, X_SWAP), go(up_p, Z_UP), go(up_m, Z_DOWN)
    s4d, s3dt, s3db, down5p, down5m, down_own = down_later(
        part, rest, hid_a, hid_b, dy_late, (d1, d2p, d2m), [bf16, bf16, f32]
    )
    d4, d3p, d3m = go(s4d, X_SWAP), go(s3dt, Z_UP), go(s3db, Z_DOWN)
    u1, u2p, u2m = after([u1, u2p, u2m], s3dt)
    s4u, s3ut, s3ub = join(up4, up3, u1, u2p, u2m, "up_join")
    u3p, u3m, u4 = go(s3ut, Z_UP), go(s3ub, Z_DOWN), go(s4u, X_SWAP)
    d3p, d3m, d4 = after([d3p, d3m, d4], s3ut)
    s5dp, s5dm = last_hop(down5p, down5m, d3p, d3m, "down_last")
    d5p, d5m = go(s5dp, Z_UP), go(s5dm, Z_DOWN)
    u3p, u3m = after([u3p, u3m], s5dp)
    s5up, s5um = last_hop(up5p, up5m, u3p, u3m, "up_last")
    u5p, u5m = go(s5up, Z_UP), go(s5um, Z_DOWN)

    d5p, d5m, u4 = after([d5p, d5m, u4], s5up)
    kept_d, kept_u, other = totals(scalars, (down_own, d4, d5p, d5m), (up_own, u4, u5p, u5m))
    other = go(other, CORE_SWAP)
    down_update, up_update = updates(scalars, kept_d, kept_u, other, noise_down, noise_up)
    return (up_update, down_update)


def solution(mesh):
    in_specs = (
        P("dp", None),
        P("dp", "tensor"),
        P("dp", "tensor"),
        P("dp", None),
        P("dp", "tensor"),
        P("dp", "tensor"),
        P("dp", "tensor"),
    )
    out_specs = (P("dp", "tensor"), P("dp", "tensor"))
    return jax.shard_map(
        on_device, mesh=mesh, in_specs=in_specs, out_specs=out_specs, check_vma=False
    )
```

```python
import functools
import math

import jax
import jax.numpy as jnp
from jax import lax
from jax.experimental import pallas as pl
from jax.experimental.pallas import tpu as pltpu
from jax.sharding import PartitionSpec as P

D = 2304
FF = 18432
SEQ = 384
N_DP = 16
N_TENSOR = 8
COST = pl.CostEstimate(flops=1000, bytes_accessed=1000, transcendentals=0)

Z_UP = [(i, (i + 4) % 16) for i in range(16)]
Z_DOWN = [(i, (i + 12) % 16) for i in range(16)]
X_SWAP = [(i, i ^ 2) for i in range(16)]
CORE_SWAP = [(i, i ^ 1) for i in range(16)]
TENSOR_SWAPS = [[(t, t ^ k) for t in range(8)] for k in (4, 1, 3)]


VMEM = pl.BlockSpec(memory_space=pltpu.VMEM)
SMEM = pl.BlockSpec(memory_space=pltpu.SMEM)
HBM = pl.BlockSpec(memory_space=pl.ANY)


def in_vmem(a):
    return pltpu.with_memory_space_constraint(a, pltpu.VMEM)


def in_hbm(a):
    return pltpu.with_memory_space_constraint(a, pltpu.HBM)


def nt(a, b):
    return lax.dot_general(a, b, (((1,), (1,)), ((), ())), preferred_element_type=jnp.float32)


def nn(a, b):
    return lax.dot_general(a, b, (((1,), (0,)), ((), ())), preferred_element_type=jnp.float32)


def tn(a, b):
    return lax.dot_general(a, b, (((0,), (0,)), ((), ())), preferred_element_type=jnp.float32)


def call(kernel, name, in_specs, out_specs, out_shape, scratch=(), mib=21):
    return pl.pallas_call(
        kernel,
        in_specs=in_specs,
        out_specs=out_specs,
        out_shape=out_shape,
        scratch_shapes=list(scratch),
        compiler_params=pltpu.CompilerParams(vmem_limit_bytes=mib << 20),
        cost_estimate=COST,
        name=name,
    )


def rows_of(e):
    return pl.ds(e * SEQ, SEQ)


def chunk(s_ref, j, ref):
    rows = ref.shape[0] // 8
    return pl.ds(pl.multiple_of(s_ref[j] * rows, 32), rows)


def turn(x_ref, dy_ref, xt_ref, dyt_ref, gx_ref, gdy_ref, arrivals):
    for e in range(2):
        arrivals[2 * e].wait()
        x = x_ref[rows_of(e), :]
        xt_ref[:, rows_of(e)] = x.T
        gx_ref[e] = nt(x, x)
        arrivals[2 * e + 1].wait()
        dy = dy_ref[rows_of(e), :]
        dyt_ref[:, rows_of(e)] = dy.T
        gdy_ref[e] = nt(dy, dy)


def token_copies(x_hbm, dy_hbm, x_ref, dy_ref, sems):
    pairs = []
    for e in range(2):
        for src, dst in ((x_hbm, x_ref), (dy_hbm, dy_ref)):
            pairs.append((src.at[rows_of(e), :], dst.at[rows_of(e), :]))
    return [pltpu.make_async_copy(src, dst, sems.at[j]) for j, (src, dst) in enumerate(pairs)]


def hidden_norm(gate_ref, up_ref, gdy_ref, hid_ref, vd_ref):
    at = lax.broadcasted_iota(jnp.int32, vd_ref.shape, 0)
    value = jnp.zeros(vd_ref.shape, jnp.float32)
    for e in range(2):
        gate, up = gate_ref[rows_of(e), :].astype(jnp.float32), up_ref[rows_of(e), :].astype(jnp.float32)
        hid = (gate * up).astype(jnp.bfloat16)
        hid_ref[rows_of(e), :] = hid
        value += jnp.where(at == e, jnp.sum(gdy_ref[e] * nt(hid, hid)), 0.0)
    vd_ref[...] = value


def own_kernel(
    s_ref, x_hbm, dy_hbm, gate_hbm, up_hbm, xt_hbm, dyt_ref, gx_hbm, gate_ref, hid_ref, vd_ref, sent_ref,
    x_ref, dy_ref, xt_ref, up_ref, gx_ref, gdy_ref, sems,
):
    tok, ff = hid_ref.shape
    tokens = token_copies(x_hbm, dy_hbm, x_ref, dy_ref, sems)
    mine = pl.ds(pl.multiple_of(s_ref[8] * ff, 128), ff)
    other = pl.ds(pl.multiple_of((1 - s_ref[8]) * ff, 128), ff)
    pairs = [
        (gate_hbm.at[:, mine], gate_ref),
        (up_hbm.at[:, mine], up_ref),
        (gate_hbm.at[:, other], sent_ref.at[pl.ds(0, tok), :]),
        (up_hbm.at[:, other], sent_ref.at[pl.ds(tok, tok), :]),
    ]
    columns = [pltpu.make_async_copy(src, dst, sems.at[4 + j]) for j, (src, dst) in enumerate(pairs)]
    for copy in tokens + columns:
        copy.start()
    turn(x_ref, dy_ref, xt_ref, dyt_ref, gx_ref, gdy_ref, tokens)
    keep = [pltpu.make_async_copy(gx_ref, gx_hbm, sems.at[8]), pltpu.make_async_copy(xt_ref, xt_hbm, sems.at[9])]
    for copy in keep:
        copy.start()
    columns[0].wait()
    columns[1].wait()
    hidden_norm(gate_ref, up_ref, gdy_ref, hid_ref, vd_ref)
    for copy in columns[2:] + keep:
        copy.wait()


def prep_own(scalars, x, dy, gate, up, ff):
    tok, width = x.shape
    bf16, f32 = jnp.bfloat16, jnp.float32
    cols = pltpu.VMEM((tok, ff), bf16)
    gram = (2, SEQ, SEQ)
    return call(
        own_kernel,
        "prep_own",
        [SMEM] + [HBM] * 4,
        [HBM, VMEM, HBM] + [VMEM] * 4,
        [
            pltpu.HBM((width, tok), bf16),
            pltpu.VMEM((width, tok), bf16),
            pltpu.HBM(gram, f32),
            cols,
            cols,
            jax.ShapeDtypeStruct((8, 128), f32),
            pltpu.VMEM((2 * tok, ff), bf16),
        ],
        [pltpu.VMEM((tok, width), bf16)] * 2
        + [pltpu.VMEM((width, tok), bf16), cols, pltpu.VMEM(gram, f32), pltpu.VMEM(gram, f32)]
        + [pltpu.SemaphoreType.DMA((10,))],
    )(scalars, *[in_hbm(a) for a in (x, dy, gate, up)])


def other_kernel(x_hbm, dy_hbm, xt_hbm, dyt_ref, gx_hbm, gdy_ref, x_ref, dy_ref, xt_ref, gx_ref, sems):
    tokens = token_copies(x_hbm, dy_hbm, x_ref, dy_ref, sems)
    for copy in tokens:
        copy.start()
    turn(x_ref, dy_ref, xt_ref, dyt_ref, gx_ref, gdy_ref, tokens)
    keep = [pltpu.make_async_copy(gx_ref, gx_hbm, sems.at[4]), pltpu.make_async_copy(xt_ref, xt_hbm, sems.at[5])]
    for copy in keep:
        copy.start()
    for copy in keep:
        copy.wait()


def prep_other(x, dy):
    tok, width = x.shape
    bf16, f32 = jnp.bfloat16, jnp.float32
    gram = (2, SEQ, SEQ)
    return call(
        other_kernel,
        "prep_other",
        [HBM] * 2,
        [HBM, VMEM, HBM, VMEM],
        [pltpu.HBM((width, tok), bf16), pltpu.VMEM((width, tok), bf16), pltpu.HBM(gram, f32), pltpu.VMEM(gram, f32)],
        [pltpu.VMEM((tok, width), bf16)] * 2
        + [pltpu.VMEM((width, tok), bf16), pltpu.VMEM(gram, f32), pltpu.SemaphoreType.DMA((6,))],
    )(in_hbm(x), in_hbm(dy))


def hidden_kernel(gu_ref, gdy_ref, hid_ref, vd_ref):
    tok = hid_ref.shape[0]
    hidden_norm(gu_ref.at[pl.ds(0, tok), :], gu_ref.at[pl.ds(tok, tok), :], gdy_ref, hid_ref, vd_ref)


def hidden_other(gu, gdy):
    tok, ff = gu.shape[0] // 2, gu.shape[1]
    return call(
        hidden_kernel,
        "hidden_other",
        [VMEM] * 2,
        [VMEM] * 2,
        [pltpu.VMEM((tok, ff), jnp.bfloat16), jax.ShapeDtypeStruct((8, 128), jnp.float32)],
    )(in_vmem(gu), in_vmem(gdy))


def halves_kernel(a_ref, b_ref, top_ref, bottom_ref, sems):
    half = top_ref.shape[0]
    copies = [
        pltpu.make_async_copy(a_ref.at[pl.ds(0, half), :], top_ref, sems.at[0]),
        pltpu.make_async_copy(b_ref.at[pl.ds(half, half), :], bottom_ref, sems.at[1]),
    ]
    for copy in copies:
        copy.start()
    for copy in copies:
        copy.wait()


def halves(a, b):
    half = pltpu.VMEM((a.shape[0] // 2, a.shape[1]), a.dtype)
    return call(halves_kernel, "halves", [HBM] * 2, [VMEM] * 2, [half, half], [pltpu.SemaphoreType.DMA((2,))])(
        in_hbm(a), in_hbm(b)
    )


def fetch(pieces, w_ref, sems):
    copies, at = [], 0
    for j, piece in enumerate(pieces):
        n = piece.shape[0]
        copies.append(pltpu.make_async_copy(piece, w_ref.at[pl.ds(at, n), :], sems.at[j]))
        at += n
    for copy in copies:
        copy.start()
    for copy in copies:
        copy.wait()


def chunks_of(s_ref, first, n, ref, columns):
    return jnp.concatenate([ref[chunk(s_ref, j, ref), columns] for j in range(first, first + n)])


def near_kernel(n, s_ref, dyt_ref, *rest):
    pieces, (out_ref, w_ref, sems) = rest[:-3], rest[-3:]
    fetch(pieces, w_ref, sems)
    for e in range(2):
        out_ref[rows_of(e), :] = tn(chunks_of(s_ref, 0, n, dyt_ref, rows_of(e)), w_ref[...])


def near(scalars, dyt, pieces, name):
    width, tok = dyt.shape
    ff, n = pieces[0].shape[1], len(pieces)
    return call(
        functools.partial(near_kernel, n),
        name,
        [SMEM, VMEM] + [HBM] * n,
        VMEM,
        pltpu.VMEM((tok, ff), jnp.float32),
        [pltpu.VMEM((width // 8 * n, ff), jnp.bfloat16), pltpu.SemaphoreType.DMA((n,))],
    )(scalars, in_vmem(dyt), *[in_hbm(a) for a in pieces])


def act_kernel(near_counts, s_ref, dya, dyb, na, nb, ga, gb, gxa_hbm, gxb_hbm, vda, vdb, *rest):
    pieces, (act_hbm_a, act_hbm_b, v_ref, w_ref, act_ref, gxa, gxb, sems) = rest[:-8], rest[-8:]
    grams = [pltpu.make_async_copy(gxa_hbm, gxa, sems.at[12]), pltpu.make_async_copy(gxb_hbm, gxb, sems.at[13])]
    for copy in grams:
        copy.start()
    fetch(pieces, w_ref, sems)
    at = lax.broadcasted_iota(jnp.int32, v_ref.shape, 0)
    value = vda[...] + pltpu.roll(vdb[...], 2, 0)
    copies = []
    depth = w_ref.shape[0]
    for half, (n, dyt, near_ref, gate, gx, act_hbm) in enumerate(
        zip(near_counts, (dya, dyb), (na, nb), (ga, gb), (gxa, gxb), (act_hbm_a, act_hbm_b))
    ):
        below = depth - dyt.shape[0] // 8 * (8 - n)
        grams[half].wait()
        w = w_ref[below:, :]
        for e in range(2):
            grad = near_ref[rows_of(e), :] + tn(chunks_of(s_ref, n, 8 - n, dyt, rows_of(e)), w)
            act = (grad * gate[rows_of(e), :].astype(jnp.float32)).astype(jnp.bfloat16)
            k = 2 * half + e
            act_ref[rows_of(k), :] = act
            copies.append(pltpu.make_async_copy(act_ref.at[rows_of(k), :], act_hbm.at[rows_of(e), :], sems.at[8 + k]))
            copies[-1].start()
            value += jnp.where(at == k, jnp.sum(gx[e] * nt(act, act)), 0.0)
    v_ref[...] = value
    for copy in copies:
        copy.wait()


def act_grads(near_counts, scalars, dyt_a, dyt_b, near_a, near_b, gate_a, gate_b, gx_a, gx_b, vd_a, vd_b, pieces):
    width, tok = dyt_a.shape
    ff = near_a.shape[1]
    grads = pltpu.HBM((tok, ff), jnp.bfloat16)
    args = [in_vmem(a) for a in (dyt_a, dyt_b, near_a, near_b, gate_a, gate_b)] + [in_hbm(gx_a), in_hbm(gx_b)]
    return call(
        functools.partial(act_kernel, near_counts),
        "act_grads",
        [SMEM] + [VMEM] * 6 + [HBM] * 2 + [VMEM] * 2 + [HBM] * len(pieces),
        [HBM, HBM, VMEM],
        [grads, grads, jax.ShapeDtypeStruct((8, 128), jnp.float32)],
        [
            pltpu.VMEM((width // 8 * (8 - min(near_counts)), ff), jnp.bfloat16),
            pltpu.VMEM((2 * tok, ff), jnp.bfloat16),
            pltpu.VMEM(gx_a.shape, gx_a.dtype),
            pltpu.VMEM(gx_b.shape, gx_b.dtype),
            pltpu.SemaphoreType.DMA((14,)),
        ],
    )(scalars, *args, vd_a, vd_b, *pieces)


def clips(p_ref, q_ref):
    bound = 4.0 * math.sqrt(D * FF)
    sq_norm = jnp.maximum(p_ref[...] + q_ref[...], 0.0)
    return bound / jnp.maximum(jnp.sqrt(sq_norm), bound)


def clip_rows(clip, first, src_ref, dst_ref):
    for e in range(2):
        at = rows_of(e)
        scale = clip[first + e : first + e + 1, :1]
        dst_ref[at, :] = (src_ref[at, :].astype(jnp.float32) * scale).astype(jnp.bfloat16)


def pair_copies(s_ref, n, a_hbm, b_hbm, dst_ref, sems, first):
    rows = dst_ref.shape[1]
    copies = []
    for k, src in enumerate((a_hbm, b_hbm)):
        for j in range(n):
            at = pl.ds(pl.multiple_of(s_ref[j] * rows, 32), rows)
            copies.append(pltpu.make_async_copy(src.at[at, :], dst_ref.at[k * n + j], sems.at[first + k * n + j]))
    return copies


def down_first_kernel(s_ref, p_ref, q_ref, la_ref, lb_ref, ra_ref, rb_ref, *rest):
    outs, (sa_ref, sb_ref, o_ref, sems) = rest[:3], rest[3:]
    clip = clips(p_ref, q_ref)
    clip_rows(clip, 0, ra_ref, sa_ref)
    clip_rows(clip, 2, rb_ref, sb_ref)
    copies = []
    for j, out in enumerate(outs):
        at = chunk(s_ref, j, la_ref)
        o_ref[j] = (nn(la_ref[at, :], sa_ref[...]) + nn(lb_ref[at, :], sb_ref[...])).astype(o_ref.dtype)
        copies.append(pltpu.make_async_copy(o_ref.at[j], out, sems.at[j]))
        copies[-1].start()
    for copy in copies:
        copy.wait()


def down_first(scalars, p, q, dyt_a, dyt_b, hid_a, hid_b):
    tok, ff = hid_a.shape
    rows = dyt_a.shape[0] // 8
    bf16 = jnp.bfloat16
    cols = pltpu.VMEM((tok, ff), bf16)
    return call(
        down_first_kernel,
        "down_first",
        [SMEM] + [VMEM] * 6,
        [HBM] * 3,
        [pltpu.HBM((rows, ff), bf16)] * 3,
        [cols, cols, pltpu.VMEM((3, rows, ff), bf16), pltpu.SemaphoreType.DMA((3,))],
    )(scalars, p, q, *[in_vmem(a) for a in (dyt_a, dyt_b, hid_a, hid_b)])


def up_all_kernel(
    dtypes, e_ref, s_ref, p_ref, q_ref, acta_hbm, actb_hbm, xta_hbm, xtb_hbm, ha_hbm, hb_hbm, dya_hbm, dyb_hbm, *rest
):
    outs, (ha_ref, hb_ref, dy_ref, x_ref, l_ref, sa_ref, sb_ref, narrow_ref, wide_ref, sems) = rest[:8], rest[8:]
    first = [
        pltpu.make_async_copy(acta_hbm, sa_ref, sems.at[30]),
        pltpu.make_async_copy(actb_hbm, sb_ref, sems.at[31]),
    ] + pair_copies(e_ref, 3, xta_hbm, xtb_hbm, x_ref, sems, 32)
    loads = pair_copies(s_ref, 5, xta_hbm, xtb_hbm, l_ref, sems, 0)
    for copy in first:
        copy.start()
    ahead = [
        pltpu.make_async_copy(ha_hbm, ha_ref, sems.at[10]),
        pltpu.make_async_copy(hb_hbm, hb_ref, sems.at[11]),
    ] + pair_copies(s_ref, 5, dya_hbm, dyb_hbm, dy_ref, sems, 12)
    clip = clips(p_ref, q_ref)
    first[0].wait()
    clip_rows(clip, 0, sa_ref, sa_ref)
    first[1].wait()
    clip_rows(clip, 2, sb_ref, sb_ref)
    for copy in first[2:]:
        copy.wait()
    for copy in loads:
        copy.start()
    stores = {jnp.float32: [], jnp.bfloat16: []}
    for j, (dtype, out) in enumerate(zip(dtypes, outs)):
        if j == 3:
            for copy in loads:
                copy.wait()
            for copy in ahead:
                copy.start()
        a, b = (x_ref[j], x_ref[3 + j]) if j < 3 else (l_ref[j - 3], l_ref[j + 2])
        earlier = stores[dtype]
        held = (wide_ref if dtype == jnp.float32 else narrow_ref).at[len(earlier)]
        held[...] = (nn(a, sa_ref[...]) + nn(b, sb_ref[...])).astype(dtype)
        earlier.append(pltpu.make_async_copy(held, out, sems.at[22 + j]))
        earlier[-1].start()
    for copy in ahead + stores[jnp.float32] + stores[jnp.bfloat16]:
        copy.wait()


def up_all(early, late_chunks, p, q, act_a, act_b, xt_a, xt_b, hid_a, hid_b, dyt_a, dyt_b, dtypes):
    tok, ff = act_a.shape
    rows = xt_a.shape[0] // 8
    bf16 = jnp.bfloat16
    cols = pltpu.VMEM((tok, ff), bf16)
    late = pltpu.VMEM((10, rows, tok), bf16)
    wide = sum(dtype == jnp.float32 for dtype in dtypes)
    return call(
        functools.partial(up_all_kernel, dtypes),
        "up_all",
        [SMEM] * 2 + [VMEM] * 2 + [HBM] * 8,
        [HBM] * 8 + [VMEM] * 3,
        [pltpu.HBM((rows, ff), dtype) for dtype in dtypes] + [cols, cols, late],
        [pltpu.VMEM((6, rows, tok), bf16), late, cols, cols, pltpu.VMEM((8 - wide, rows, ff), bf16), pltpu.VMEM((wide, rows, ff), jnp.float32)]
        + [pltpu.SemaphoreType.DMA((38,))],
        26,
    )(early, late_chunks, p, q, *[in_hbm(a) for a in (act_a, act_b, xt_a, xt_b, hid_a, hid_b, dyt_a, dyt_b)])


def down_later_kernel(p_ref, q_ref, ha_ref, hb_ref, dy_ref, *rest):
    got_hbm, outs, got_refs, (sa_ref, sb_ref, sems) = rest[:3], rest[3:9], rest[9:12], rest[12:]
    got = [pltpu.make_async_copy(src, dst, sems.at[j]) for j, (src, dst) in enumerate(zip(got_hbm, got_refs))]
    for copy in got:
        copy.start()
    clip = clips(p_ref, q_ref)
    clip_rows(clip, 0, ha_ref, sa_ref)
    clip_rows(clip, 2, hb_ref, sb_ref)

    def share(j):
        return nn(dy_ref[j], sa_ref[...]) + nn(dy_ref[5 + j], sb_ref[...])

    for j, out in enumerate(outs[3:]):
        out[...] = share(2 + j).astype(out.dtype)
    for copy in got:
        copy.wait()
    tree_add(share(0), share(1), *got_refs, *outs[:3])


def down_later(p, q, hid_a, hid_b, dy_late, got, dtypes):
    tok, ff = hid_a.shape
    rows = dy_late.shape[1]
    bf16 = jnp.bfloat16
    half = jax.ShapeDtypeStruct((rows // 2, ff), bf16)
    cols = pltpu.VMEM((tok, ff), bf16)
    return call(
        down_later_kernel,
        "down_later",
        [VMEM] * 5 + [HBM] * 3,
        [VMEM] * 6,
        [jax.ShapeDtypeStruct((rows, ff), bf16), half, half]
        + [jax.ShapeDtypeStruct((rows, ff), dtype) for dtype in dtypes],
        [pltpu.VMEM((rows, ff), bf16)] * 3 + [cols, cols, pltpu.SemaphoreType.DMA((3,))],
    )(p, q, *[in_vmem(a) for a in (hid_a, hid_b, dy_late)], *got)


def tree_add(m4, m3, r1_ref, r2p_ref, r2m_ref, s4_ref, top_ref, bottom_ref):
    f32, bf16 = jnp.float32, jnp.bfloat16
    half = top_ref.shape[0]
    s3 = (m3 + r1_ref[...].astype(f32)).astype(bf16)
    top_ref[...] = s3[:half]
    bottom_ref[...] = s3[half:]
    s4_ref[...] = (m4 + r2p_ref[...].astype(f32) + r2m_ref[...].astype(f32)).astype(bf16)


def take(hbm_refs, refs, sems):
    copies = [pltpu.make_async_copy(src, dst, sems.at[j]) for j, (src, dst) in enumerate(zip(hbm_refs, refs))]
    for copy in copies:
        copy.start()
    for copy in copies:
        copy.wait()


def join_kernel(*refs):
    ins, outs, (*held, sems) = refs[:5], refs[5:8], refs[8:]
    take(ins, held, sems)
    m4_ref, m3_ref, *got = held
    tree_add(m4_ref[...], m3_ref[...], *got, *outs)


def join(m4, m3, r1, r2p, r2m, name):
    rows, ff = m4.shape
    bf16 = jnp.bfloat16
    half = jax.ShapeDtypeStruct((rows // 2, ff), bf16)
    arrays = [in_hbm(m4), in_hbm(m3), r1, r2p, r2m]
    return call(
        join_kernel,
        name,
        [HBM] * 5,
        [VMEM] * 3,
        [jax.ShapeDtypeStruct((rows, ff), bf16), half, half],
        [pltpu.VMEM((rows, ff), a.dtype) for a in arrays] + [pltpu.SemaphoreType.DMA((5,))],
    )(*arrays)


def last_hop_kernel(*refs):
    hbm, (sp_ref, sm_ref), (mp_ref, mm_ref, rp_ref, rm_ref, sems) = refs[:4], refs[4:6], refs[6:]
    f32, bf16 = jnp.float32, jnp.bfloat16
    take(hbm, (mp_ref, mm_ref, rp_ref, rm_ref), sems)
    half = rp_ref.shape[0]
    upper, lower = pl.ds(0, half), pl.ds(half, half)
    sp_ref[upper, :] = (mp_ref[upper, :].astype(f32) + rp_ref[...].astype(f32)).astype(bf16)
    sp_ref[lower, :] = mp_ref[lower, :].astype(bf16)
    sm_ref[upper, :] = mm_ref[upper, :].astype(bf16)
    sm_ref[lower, :] = (mm_ref[lower, :].astype(f32) + rm_ref[...].astype(f32)).astype(bf16)


def last_hop(mp, mm, rp, rm, name):
    out = jax.ShapeDtypeStruct(mp.shape, jnp.bfloat16)
    arrays = (mp, mm, rp, rm)
    return call(
        last_hop_kernel,
        name,
        [HBM] * 4,
        [VMEM] * 2,
        [out, out],
        [pltpu.VMEM(a.shape, a.dtype) for a in arrays] + [pltpu.SemaphoreType.DMA((4,))],
    )(*arrays)


def total_kernel(s_ref, *refs):
    (down, up), (kept_d, kept_u, other_ref) = (refs[:4], refs[4:8]), refs[8:]
    half = kept_d.shape[0]
    mine = pl.ds(pl.multiple_of(s_ref[8] * half, 16), half)
    others = pl.ds(pl.multiple_of((1 - s_ref[8]) * half, 16), half)
    for (m, *got), kept, at in ((down, kept_d, 0), (up, kept_u, half)):
        for src, dst in ((mine, kept), (others, other_ref.at[pl.ds(at, half), :])):
            got4, gotp, gotm = [r[src, :].astype(jnp.float32) for r in got]
            dst[...] = (m[src, :] + got4 + gotp + gotm).astype(dst.dtype)


def totals(scalars, down, up):
    rows, ff = down[0].shape
    half = jax.ShapeDtypeStruct((rows // 2, ff), jnp.float32)
    return call(
        total_kernel,
        "totals",
        [SMEM] + [VMEM] * 8,
        [VMEM] * 3,
        [half, half, jax.ShapeDtypeStruct((rows, ff), jnp.bfloat16)],
    )(scalars, *down, *up)


def update_kernel(s_ref, kept_d, kept_u, other_ref, noise_d, noise_u, out_d, out_u):
    half, ff = kept_d.shape
    mine = pl.ds(pl.multiple_of(s_ref[8] * ff, 128), ff)
    others = pl.ds(pl.multiple_of((1 - s_ref[8]) * ff, 128), ff)
    for at, kept, noise, out in ((0, kept_d, noise_d, out_d), (half, kept_u, noise_u, out_u)):
        out[:, mine] = (kept[...] + noise[:, mine]) * (1.0 / (2 * N_DP))
        out[:, others] = (other_ref[pl.ds(at, half), :].astype(jnp.float32) + noise[:, others]) * (1.0 / (2 * N_DP))


def updates(scalars, kept_d, kept_u, other, noise_d, noise_u):
    out = jax.ShapeDtypeStruct(noise_d.shape, jnp.float32)
    return call(update_kernel, "updates", [SMEM] + [VMEM] * 5, [VMEM] * 2, [out, out])(
        scalars, kept_d, kept_u, other, noise_d, noise_u
    )


def after(values, *earlier):
    return lax.optimization_barrier((tuple(values),) + earlier)[0]


def on_device(inputs, up_pre, gate_act, out_grad, down_weight, noise_up, noise_down):
    ff = up_pre.shape[1] // 2
    own_rows = down_weight.shape[0]
    me = lax.axis_index("dp")
    core, x, z = me % 2, (me // 2) % 2, me // 4

    def chip(dz, dx):
        return ((z + dz) % 4) * 2 + ((x + dx) % 2)

    def half_cols(a, which):
        return lax.dynamic_slice(a, (0, which * ff), (a.shape[0], ff))

    def go(a, perm):
        return lax.ppermute(a, "dp", perm)

    near_chips = [chip(0, 0), chip(3, 0), chip(1, 0), chip(0, 1), chip(2, 0)]
    far_chips = [chip(3, 1), chip(1, 1), chip(2, 1)]
    scalars = jnp.stack(near_chips + far_chips + [core]).astype(jnp.int32)

    w_mine = half_cols(down_weight, core)
    w_other = go(half_cols(down_weight, 1 - core), CORE_SWAP)
    own = jnp.where(core == 0, jnp.concatenate([w_mine, w_other]), jnp.concatenate([w_other, w_mine]))
    w_x = go(own, X_SWAP)
    w_zp = go(own, Z_DOWN)
    w_zm = go(own, Z_UP)

    dy_src, x_src = after([out_grad, inputs], own)
    dy_b = go(dy_src, CORE_SWAP)
    x_b = go(x_src, CORE_SWAP)
    x_own, dy_own = after([inputs, out_grad], own)
    xt_a, dyt_a, gx_a, gate_a, hid_a, vd_a, gu_send = prep_own(scalars, x_own, dy_own, gate_act, up_pre, ff)

    x_b, dy_b = after([x_b, dy_b], vd_a)
    xt_b, dyt_b, gx_b, gdy_b = prep_other(x_b, dy_b)

    w_x, w_zp, w_zm, gu_send = after([w_x, w_zp, w_zm, gu_send], dyt_b)
    up_half, down_half = halves(w_zm, w_zp)
    w_z2_top = go(up_half, Z_UP)
    w_z2_bot = go(down_half, Z_DOWN)
    gu_b = go(gu_send, CORE_SWAP)
    w_x = after([w_x], up_half)[0]
    w_zm_x = go(w_x, Z_UP)
    w_zp_x = go(w_x, Z_DOWN)
    near_a = near(scalars, after([dyt_a], up_half)[0], [own, w_zm, w_zp, w_x], "near_own")
    w_z2_top, w_z2_bot = after([w_z2_top, w_z2_bot], near_a)
    w_z2 = jnp.concatenate([w_z2_top, w_z2_bot])
    w_z2_x = go(w_z2, X_SWAP)
    hid_b, vd_b = hidden_other(after([gu_b], w_z2)[0], gdy_b)
    near_b = near(scalars, after([dyt_b], hid_b)[0], [own, w_zm, w_zp, w_x, w_z2], "near_other")
    w_zm_x, w_zp_x, w_z2_x = after([w_zm_x, w_zp_x, w_z2_x], near_b, vd_b)
    far_pieces = [in_hbm(w_z2), w_zm_x, w_zp_x, w_z2_x]
    act_a, act_b, part = act_grads(
        (4, 5), scalars, dyt_a, dyt_b, near_a, near_b, gate_a, gu_b, gx_a, gx_b, vd_a, vd_b, far_pieces
    )

    got = go(part, CORE_SWAP)
    part = part + jnp.concatenate([got[2:4], got[0:2], got[4:]])
    for swap in TENSOR_SWAPS[:2]:
        part = part + lax.ppermute(part, "tensor", swap)
    rest = lax.ppermute(part, "tensor", TENSOR_SWAPS[2])

    early_chips = [chip(1, 1), chip(3, 1), chip(2, 1)]
    late_chips = [chip(0, 1), chip(2, 0), chip(1, 0), chip(3, 0), chip(0, 0)]
    early = jnp.stack(early_chips).astype(jnp.int32)
    late = jnp.stack(late_chips).astype(jnp.int32)

    f32, bf16 = jnp.float32, jnp.bfloat16
    down_p, down_m, down_x = down_first(early, part, rest, dyt_a, dyt_b, hid_a, hid_b)
    d1, d2p, d2m = go(down_x, X_SWAP), go(down_p, Z_UP), go(down_m, Z_DOWN)
    up_p, up_m, up_x, up4, up3, up5p, up5m, up_own, hid_a, hid_b, dy_late = up_all(
        early, late, part, rest, *after([act_a, act_b], down_x), xt_a, xt_b, hid_a, hid_b, dyt_a, dyt_b,
        [bf16] * 3 + [f32, f32, bf16, bf16, f32],
    )
    d1, d2p, d2m = after([d1, d2p, d2m], up_x)
    u1, u2p, u2m = go(up_x, X_SWAP), go(up_p, Z_UP), go(up_m, Z_DOWN)
    s4d, s3dt, s3db, down5p, down5m, down_own = down_later(
        part, rest, hid_a, hid_b, dy_late, (d1, d2p, d2m), [bf16, bf16, f32]
    )
    d4, d3p, d3m = go(s4d, X_SWAP), go(s3dt, Z_UP), go(s3db, Z_DOWN)
    u1, u2p, u2m = after([u1, u2p, u2m], s3dt)
    s4u, s3ut, s3ub = join(up4, up3, u1, u2p, u2m, "up_join")
    u3p, u3m, u4 = go(s3ut, Z_UP), go(s3ub, Z_DOWN), go(s4u, X_SWAP)
    d3p, d3m, d4 = after([d3p, d3m, d4], s3ut)
    s5dp, s5dm = last_hop(down5p, down5m, d3p, d3m, "down_last")
    d5p, d5m = go(s5dp, Z_UP), go(s5dm, Z_DOWN)
    u3p, u3m = after([u3p, u3m], s5dp)
    s5up, s5um = last_hop(up5p, up5m, u3p, u3m, "up_last")
    u5p, u5m = go(s5up, Z_UP), go(s5um, Z_DOWN)

    d5p, d5m, u4 = after([d5p, d5m, u4], s5up)
    kept_d, kept_u, other = totals(scalars, (down_own, d4, d5p, d5m), (up_own, u4, u5p, u5m))
    other = go(other, CORE_SWAP)
    down_update, up_update = updates(scalars, kept_d, kept_u, other, noise_down, noise_up)
    return (up_update, down_update)


def solution(mesh):
    in_specs = (
        P("dp", None),
        P("dp", "tensor"),
        P("dp", "tensor"),
        P("dp", None),
        P("dp", "tensor"),
        P("dp", "tensor"),
        P("dp", "tensor"),
    )
    out_specs = (P("dp", "tensor"), P("dp", "tensor"))
    return jax.shard_map(
        on_device, mesh=mesh, in_specs=in_specs, out_specs=out_specs, check_vma=False
    )
```

```python
import functools
import math

import jax
import jax.numpy as jnp
from jax import lax
from jax.experimental import pallas as pl
from jax.experimental.pallas import tpu as pltpu
from jax.sharding import PartitionSpec as P

D = 2304
FF = 18432
SEQ = 384
N_DP = 16
N_TENSOR = 8
COST = pl.CostEstimate(flops=1000, bytes_accessed=1000, transcendentals=0)

Z_UP = [(i, (i + 4) % 16) for i in range(16)]
Z_DOWN = [(i, (i + 12) % 16) for i in range(16)]
X_SWAP = [(i, i ^ 2) for i in range(16)]
CORE_SWAP = [(i, i ^ 1) for i in range(16)]
TENSOR_SWAPS = [[(t, t ^ k) for t in range(8)] for k in (4, 1, 3)]


VMEM = pl.BlockSpec(memory_space=pltpu.VMEM)
SMEM = pl.BlockSpec(memory_space=pltpu.SMEM)
HBM = pl.BlockSpec(memory_space=pl.ANY)


def in_vmem(a):
    return pltpu.with_memory_space_constraint(a, pltpu.VMEM)


def in_hbm(a):
    return pltpu.with_memory_space_constraint(a, pltpu.HBM)


def nt(a, b):
    return lax.dot_general(a, b, (((1,), (1,)), ((), ())), preferred_element_type=jnp.float32)


def nn(a, b):
    return lax.dot_general(a, b, (((1,), (0,)), ((), ())), preferred_element_type=jnp.float32)


def tn(a, b):
    return lax.dot_general(a, b, (((0,), (0,)), ((), ())), preferred_element_type=jnp.float32)


def call(kernel, name, in_specs, out_specs, out_shape, scratch=(), mib=21):
    return pl.pallas_call(
        kernel,
        in_specs=in_specs,
        out_specs=out_specs,
        out_shape=out_shape,
        scratch_shapes=list(scratch),
        compiler_params=pltpu.CompilerParams(vmem_limit_bytes=mib << 20),
        cost_estimate=COST,
        name=name,
    )


def rows_of(e):
    return pl.ds(e * SEQ, SEQ)


def chunk(s_ref, j, ref):
    rows = ref.shape[0] // 8
    return pl.ds(pl.multiple_of(s_ref[j] * rows, 32), rows)


def turn(x_ref, dy_ref, xt_ref, dyt_ref, gx_ref, gdy_ref, arrivals):
    for e in range(2):
        arrivals[2 * e].wait()
        x = x_ref[rows_of(e), :]
        xt_ref[:, rows_of(e)] = x.T
        gx_ref[e] = nt(x, x)
        arrivals[2 * e + 1].wait()
        dy = dy_ref[rows_of(e), :]
        dyt_ref[:, rows_of(e)] = dy.T
        gdy_ref[e] = nt(dy, dy)


def token_copies(x_hbm, dy_hbm, x_ref, dy_ref, sems):
    pairs = []
    for e in range(2):
        for src, dst in ((x_hbm, x_ref), (dy_hbm, dy_ref)):
            pairs.append((src.at[rows_of(e), :], dst.at[rows_of(e), :]))
    return [pltpu.make_async_copy(src, dst, sems.at[j]) for j, (src, dst) in enumerate(pairs)]


def hidden_norm(gate_ref, up_ref, gdy_ref, hid_ref, vd_ref):
    at = lax.broadcasted_iota(jnp.int32, vd_ref.shape, 0)
    value = jnp.zeros(vd_ref.shape, jnp.float32)
    for e in range(2):
        gate, up = gate_ref[rows_of(e), :].astype(jnp.float32), up_ref[rows_of(e), :].astype(jnp.float32)
        hid = (gate * up).astype(jnp.bfloat16)
        hid_ref[rows_of(e), :] = hid
        value += jnp.where(at == e, jnp.sum(gdy_ref[e] * nt(hid, hid)), 0.0)
    vd_ref[...] = value


def own_kernel(
    s_ref, x_hbm, dy_hbm, gate_hbm, up_hbm, xt_hbm, dyt_ref, gx_hbm, gate_ref, hid_ref, vd_ref, sent_ref,
    x_ref, dy_ref, xt_ref, up_ref, gx_ref, gdy_ref, sems,
):
    tok, ff = hid_ref.shape
    tokens = token_copies(x_hbm, dy_hbm, x_ref, dy_ref, sems)
    mine = pl.ds(pl.multiple_of(s_ref[8] * ff, 128), ff)
    other = pl.ds(pl.multiple_of((1 - s_ref[8]) * ff, 128), ff)
    pairs = [
        (gate_hbm.at[:, mine], gate_ref),
        (up_hbm.at[:, mine], up_ref),
        (gate_hbm.at[:, other], sent_ref.at[pl.ds(0, tok), :]),
        (up_hbm.at[:, other], sent_ref.at[pl.ds(tok, tok), :]),
    ]
    columns = [pltpu.make_async_copy(src, dst, sems.at[4 + j]) for j, (src, dst) in enumerate(pairs)]
    for copy in tokens + columns:
        copy.start()
    turn(x_ref, dy_ref, xt_ref, dyt_ref, gx_ref, gdy_ref, tokens)
    keep = [pltpu.make_async_copy(gx_ref, gx_hbm, sems.at[8]), pltpu.make_async_copy(xt_ref, xt_hbm, sems.at[9])]
    for copy in keep:
        copy.start()
    columns[0].wait()
    columns[1].wait()
    hidden_norm(gate_ref, up_ref, gdy_ref, hid_ref, vd_ref)
    for copy in columns[2:] + keep:
        copy.wait()


def prep_own(scalars, x, dy, gate, up, ff):
    tok, width = x.shape
    bf16, f32 = jnp.bfloat16, jnp.float32
    cols = pltpu.VMEM((tok, ff), bf16)
    gram = (2, SEQ, SEQ)
    return call(
        own_kernel,
        "prep_own",
        [SMEM] + [HBM] * 4,
        [HBM, VMEM, HBM] + [VMEM] * 4,
        [
            pltpu.HBM((width, tok), bf16),
            pltpu.VMEM((width, tok), bf16),
            pltpu.HBM(gram, f32),
            cols,
            cols,
            jax.ShapeDtypeStruct((8, 128), f32),
            pltpu.VMEM((2 * tok, ff), bf16),
        ],
        [pltpu.VMEM((tok, width), bf16)] * 2
        + [pltpu.VMEM((width, tok), bf16), cols, pltpu.VMEM(gram, f32), pltpu.VMEM(gram, f32)]
        + [pltpu.SemaphoreType.DMA((10,))],
    )(scalars, *[in_hbm(a) for a in (x, dy, gate, up)])


def other_kernel(x_hbm, dy_hbm, xt_hbm, dyt_ref, gx_hbm, gdy_ref, x_ref, dy_ref, xt_ref, gx_ref, sems):
    tokens = token_copies(x_hbm, dy_hbm, x_ref, dy_ref, sems)
    for copy in tokens:
        copy.start()
    turn(x_ref, dy_ref, xt_ref, dyt_ref, gx_ref, gdy_ref, tokens)
    keep = [pltpu.make_async_copy(gx_ref, gx_hbm, sems.at[4]), pltpu.make_async_copy(xt_ref, xt_hbm, sems.at[5])]
    for copy in keep:
        copy.start()
    for copy in keep:
        copy.wait()


def prep_other(x, dy):
    tok, width = x.shape
    bf16, f32 = jnp.bfloat16, jnp.float32
    gram = (2, SEQ, SEQ)
    return call(
        other_kernel,
        "prep_other",
        [HBM] * 2,
        [HBM, VMEM, HBM, VMEM],
        [pltpu.HBM((width, tok), bf16), pltpu.VMEM((width, tok), bf16), pltpu.HBM(gram, f32), pltpu.VMEM(gram, f32)],
        [pltpu.VMEM((tok, width), bf16)] * 2
        + [pltpu.VMEM((width, tok), bf16), pltpu.VMEM(gram, f32), pltpu.SemaphoreType.DMA((6,))],
    )(in_hbm(x), in_hbm(dy))


def hidden_kernel(gu_ref, gdy_ref, hid_ref, vd_ref):
    tok = hid_ref.shape[0]
    hidden_norm(gu_ref.at[pl.ds(0, tok), :], gu_ref.at[pl.ds(tok, tok), :], gdy_ref, hid_ref, vd_ref)


def hidden_other(gu, gdy):
    tok, ff = gu.shape[0] // 2, gu.shape[1]
    return call(
        hidden_kernel,
        "hidden_other",
        [VMEM] * 2,
        [VMEM] * 2,
        [pltpu.VMEM((tok, ff), jnp.bfloat16), jax.ShapeDtypeStruct((8, 128), jnp.float32)],
    )(in_vmem(gu), in_vmem(gdy))


def halves_kernel(a_ref, b_ref, top_ref, bottom_ref, sems):
    half = top_ref.shape[0]
    copies = [
        pltpu.make_async_copy(a_ref.at[pl.ds(0, half), :], top_ref, sems.at[0]),
        pltpu.make_async_copy(b_ref.at[pl.ds(half, half), :], bottom_ref, sems.at[1]),
    ]
    for copy in copies:
        copy.start()
    for copy in copies:
        copy.wait()


def halves(a, b):
    half = pltpu.VMEM((a.shape[0] // 2, a.shape[1]), a.dtype)
    return call(halves_kernel, "halves", [HBM] * 2, [VMEM] * 2, [half, half], [pltpu.SemaphoreType.DMA((2,))])(
        in_hbm(a), in_hbm(b)
    )


def fetch(pieces, w_ref, sems):
    copies, at = [], 0
    for j, piece in enumerate(pieces):
        n = piece.shape[0]
        copies.append(pltpu.make_async_copy(piece, w_ref.at[pl.ds(at, n), :], sems.at[j]))
        at += n
    for copy in copies:
        copy.start()
    for copy in copies:
        copy.wait()


def chunks_of(s_ref, first, n, ref, columns):
    return jnp.concatenate([ref[chunk(s_ref, j, ref), columns] for j in range(first, first + n)])


def near_kernel(n, s_ref, dyt_ref, *rest):
    pieces, (out_ref, w_ref, sems) = rest[:-3], rest[-3:]
    fetch(pieces, w_ref, sems)
    for e in range(2):
        out_ref[rows_of(e), :] = tn(chunks_of(s_ref, 0, n, dyt_ref, rows_of(e)), w_ref[...])


def near(scalars, dyt, pieces, name):
    width, tok = dyt.shape
    ff, n = pieces[0].shape[1], len(pieces)
    return call(
        functools.partial(near_kernel, n),
        name,
        [SMEM, VMEM] + [HBM] * n,
        VMEM,
        pltpu.VMEM((tok, ff), jnp.float32),
        [pltpu.VMEM((width // 8 * n, ff), jnp.bfloat16), pltpu.SemaphoreType.DMA((n,))],
    )(scalars, in_vmem(dyt), *[in_hbm(a) for a in pieces])


def act_kernel(near_counts, s_ref, dya, dyb, na, nb, ga, gb, gxa_hbm, gxb_hbm, vda, vdb, *rest):
    pieces, (act_hbm_a, act_hbm_b, v_ref, w_ref, act_ref, gxa, gxb, sems) = rest[:-8], rest[-8:]
    grams = [pltpu.make_async_copy(gxa_hbm, gxa, sems.at[12]), pltpu.make_async_copy(gxb_hbm, gxb, sems.at[13])]
    for copy in grams:
        copy.start()
    fetch(pieces, w_ref, sems)
    at = lax.broadcasted_iota(jnp.int32, v_ref.shape, 0)
    value = vda[...] + pltpu.roll(vdb[...], 2, 0)
    copies = []
    depth = w_ref.shape[0]
    for half, (n, dyt, near_ref, gate, gx, act_hbm) in enumerate(
        zip(near_counts, (dya, dyb), (na, nb), (ga, gb), (gxa, gxb), (act_hbm_a, act_hbm_b))
    ):
        below = depth - dyt.shape[0] // 8 * (8 - n)
        grams[half].wait()
        w = w_ref[below:, :]
        for e in range(2):
            grad = near_ref[rows_of(e), :] + tn(chunks_of(s_ref, n, 8 - n, dyt, rows_of(e)), w)
            act = (grad * gate[rows_of(e), :].astype(jnp.float32)).astype(jnp.bfloat16)
            k = 2 * half + e
            act_ref[rows_of(k), :] = act
            copies.append(pltpu.make_async_copy(act_ref.at[rows_of(k), :], act_hbm.at[rows_of(e), :], sems.at[8 + k]))
            copies[-1].start()
            value += jnp.where(at == k, jnp.sum(gx[e] * nt(act, act)), 0.0)
    v_ref[...] = value
    for copy in copies:
        copy.wait()


def act_grads(near_counts, scalars, dyt_a, dyt_b, near_a, near_b, gate_a, gate_b, gx_a, gx_b, vd_a, vd_b, pieces):
    width, tok = dyt_a.shape
    ff = near_a.shape[1]
    grads = pltpu.HBM((tok, ff), jnp.bfloat16)
    args = [in_vmem(a) for a in (dyt_a, dyt_b, near_a, near_b, gate_a, gate_b)] + [in_hbm(gx_a), in_hbm(gx_b)]
    return call(
        functools.partial(act_kernel, near_counts),
        "act_grads",
        [SMEM] + [VMEM] * 6 + [HBM] * 2 + [VMEM] * 2 + [HBM] * len(pieces),
        [HBM, HBM, VMEM],
        [grads, grads, jax.ShapeDtypeStruct((8, 128), jnp.float32)],
        [
            pltpu.VMEM((width // 8 * (8 - min(near_counts)), ff), jnp.bfloat16),
            pltpu.VMEM((2 * tok, ff), jnp.bfloat16),
            pltpu.VMEM(gx_a.shape, gx_a.dtype),
            pltpu.VMEM(gx_b.shape, gx_b.dtype),
            pltpu.SemaphoreType.DMA((14,)),
        ],
    )(scalars, *args, vd_a, vd_b, *pieces)


def clips(p_ref, q_ref):
    bound = 4.0 * math.sqrt(D * FF)
    sq_norm = jnp.maximum(p_ref[...] + q_ref[...], 0.0)
    return bound / jnp.maximum(jnp.sqrt(sq_norm), bound)


def clip_rows(clip, first, src_ref, dst_ref):
    for e in range(2):
        at = rows_of(e)
        scale = clip[first + e : first + e + 1, :1]
        dst_ref[at, :] = (src_ref[at, :].astype(jnp.float32) * scale).astype(jnp.bfloat16)


def pair_copies(s_ref, n, a_hbm, b_hbm, dst_ref, sems, first):
    rows = dst_ref.shape[1]
    copies = []
    for k, src in enumerate((a_hbm, b_hbm)):
        for j in range(n):
            at = pl.ds(pl.multiple_of(s_ref[j] * rows, 32), rows)
            copies.append(pltpu.make_async_copy(src.at[at, :], dst_ref.at[k * n + j], sems.at[first + k * n + j]))
    return copies


def down_first_kernel(s_ref, p_ref, q_ref, la_ref, lb_ref, ra_ref, rb_ref, *rest):
    outs, (sa_ref, sb_ref, o_ref, sems) = rest[:3], rest[3:]
    clip = clips(p_ref, q_ref)
    clip_rows(clip, 0, ra_ref, sa_ref)
    clip_rows(clip, 2, rb_ref, sb_ref)
    copies = []
    for j, out in enumerate(outs):
        at = chunk(s_ref, j, la_ref)
        o_ref[j] = (nn(la_ref[at, :], sa_ref[...]) + nn(lb_ref[at, :], sb_ref[...])).astype(o_ref.dtype)
        copies.append(pltpu.make_async_copy(o_ref.at[j], out, sems.at[j]))
        copies[-1].start()
    for copy in copies:
        copy.wait()


def down_first(scalars, p, q, dyt_a, dyt_b, hid_a, hid_b):
    tok, ff = hid_a.shape
    rows = dyt_a.shape[0] // 8
    bf16 = jnp.bfloat16
    cols = pltpu.VMEM((tok, ff), bf16)
    return call(
        down_first_kernel,
        "down_first",
        [SMEM] + [VMEM] * 6,
        [HBM] * 3,
        [pltpu.HBM((rows, ff), bf16)] * 3,
        [cols, cols, pltpu.VMEM((3, rows, ff), bf16), pltpu.SemaphoreType.DMA((3,))],
    )(scalars, p, q, *[in_vmem(a) for a in (dyt_a, dyt_b, hid_a, hid_b)])


def up_first_kernel(s_ref, p_ref, q_ref, acta_hbm, actb_hbm, xta_hbm, xtb_hbm, *rest):
    outs, (x_ref, sa_ref, sb_ref, o_ref, sems) = rest[:3], rest[3:]
    loads = [
        pltpu.make_async_copy(acta_hbm, sa_ref, sems.at[0]),
        pltpu.make_async_copy(actb_hbm, sb_ref, sems.at[1]),
    ] + pair_copies(s_ref, 3, xta_hbm, xtb_hbm, x_ref, sems, 2)
    for copy in loads:
        copy.start()
    clip = clips(p_ref, q_ref)
    loads[0].wait()
    clip_rows(clip, 0, sa_ref, sa_ref)
    loads[1].wait()
    clip_rows(clip, 2, sb_ref, sb_ref)
    for copy in loads[2:]:
        copy.wait()
    stores = []
    for j, out in enumerate(outs):
        o_ref[j] = (nn(x_ref[j], sa_ref[...]) + nn(x_ref[3 + j], sb_ref[...])).astype(o_ref.dtype)
        stores.append(pltpu.make_async_copy(o_ref.at[j], out, sems.at[8 + j]))
        stores[-1].start()
    for copy in stores:
        copy.wait()


def up_first(scalars, p, q, act_a, act_b, xt_a, xt_b):
    tok, ff = act_a.shape
    rows = xt_a.shape[0] // 8
    bf16 = jnp.bfloat16
    cols = pltpu.VMEM((tok, ff), bf16)
    return call(
        up_first_kernel,
        "up_first",
        [SMEM] + [VMEM] * 2 + [HBM] * 4,
        [HBM] * 3,
        [pltpu.HBM((rows, ff), bf16)] * 3,
        [pltpu.VMEM((6, rows, tok), bf16), cols, cols, pltpu.VMEM((3, rows, ff), bf16), pltpu.SemaphoreType.DMA((11,))],
    )(scalars, p, q, *[in_hbm(a) for a in (act_a, act_b, xt_a, xt_b)])


def up_all_kernel(
    dtypes, s_ref, p_ref, q_ref, acta_hbm, actb_hbm, xta_hbm, xtb_hbm, ha_hbm, hb_hbm, dya_hbm, dyb_hbm, *rest
):
    outs, (ha_ref, hb_ref, dy_ref, l_ref, sa_ref, sb_ref, narrow_ref, wide_ref, sems) = rest[:5], rest[5:]
    first = [
        pltpu.make_async_copy(acta_hbm, sa_ref, sems.at[30]),
        pltpu.make_async_copy(actb_hbm, sb_ref, sems.at[31]),
    ]
    loads = pair_copies(s_ref, 5, xta_hbm, xtb_hbm, l_ref, sems, 0)
    for copy in first + loads:
        copy.start()
    ahead = [
        pltpu.make_async_copy(ha_hbm, ha_ref, sems.at[10]),
        pltpu.make_async_copy(hb_hbm, hb_ref, sems.at[11]),
    ] + pair_copies(s_ref, 5, dya_hbm, dyb_hbm, dy_ref, sems, 12)
    clip = clips(p_ref, q_ref)
    first[0].wait()
    clip_rows(clip, 0, sa_ref, sa_ref)
    first[1].wait()
    clip_rows(clip, 2, sb_ref, sb_ref)
    stores = {jnp.float32: [], jnp.bfloat16: []}
    for j, (dtype, out) in enumerate(zip(dtypes, outs)):
        if j == 0:
            for copy in loads:
                copy.wait()
            for copy in ahead:
                copy.start()
        a, b = l_ref[j], l_ref[5 + j]
        earlier = stores[dtype]
        held = (wide_ref if dtype == jnp.float32 else narrow_ref).at[len(earlier)]
        held[...] = (nn(a, sa_ref[...]) + nn(b, sb_ref[...])).astype(dtype)
        earlier.append(pltpu.make_async_copy(held, out, sems.at[22 + j]))
        earlier[-1].start()
    for copy in ahead + stores[jnp.float32] + stores[jnp.bfloat16]:
        copy.wait()


def up_all(late_chunks, p, q, act_a, act_b, xt_a, xt_b, hid_a, hid_b, dyt_a, dyt_b, dtypes):
    tok, ff = act_a.shape
    rows = xt_a.shape[0] // 8
    bf16 = jnp.bfloat16
    cols = pltpu.VMEM((tok, ff), bf16)
    late = pltpu.VMEM((10, rows, tok), bf16)
    wide = sum(dtype == jnp.float32 for dtype in dtypes)
    return call(
        functools.partial(up_all_kernel, dtypes),
        "up_all",
        [SMEM] + [VMEM] * 2 + [HBM] * 8,
        [HBM] * 5 + [VMEM] * 3,
        [pltpu.HBM((rows, ff), dtype) for dtype in dtypes] + [cols, cols, late],
        [late, cols, cols, pltpu.VMEM((5 - wide, rows, ff), bf16), pltpu.VMEM((wide, rows, ff), jnp.float32)]
        + [pltpu.SemaphoreType.DMA((38,))],
        26,
    )(late_chunks, p, q, *[in_hbm(a) for a in (act_a, act_b, xt_a, xt_b, hid_a, hid_b, dyt_a, dyt_b)])


def down_later_kernel(p_ref, q_ref, ha_ref, hb_ref, dy_ref, *rest):
    got_hbm, outs, got_refs, (sa_ref, sb_ref, sems) = rest[:3], rest[3:9], rest[9:12], rest[12:]
    got = [pltpu.make_async_copy(src, dst, sems.at[j]) for j, (src, dst) in enumerate(zip(got_hbm, got_refs))]
    for copy in got:
        copy.start()
    clip = clips(p_ref, q_ref)
    clip_rows(clip, 0, ha_ref, sa_ref)
    clip_rows(clip, 2, hb_ref, sb_ref)

    def share(j):
        return nn(dy_ref[j], sa_ref[...]) + nn(dy_ref[5 + j], sb_ref[...])

    for j, out in enumerate(outs[3:]):
        out[...] = share(2 + j).astype(out.dtype)
    for copy in got:
        copy.wait()
    tree_add(share(0), share(1), *got_refs, *outs[:3])


def down_later(p, q, hid_a, hid_b, dy_late, got, dtypes):
    tok, ff = hid_a.shape
    rows = dy_late.shape[1]
    bf16 = jnp.bfloat16
    half = jax.ShapeDtypeStruct((rows // 2, ff), bf16)
    cols = pltpu.VMEM((tok, ff), bf16)
    return call(
        down_later_kernel,
        "down_later",
        [VMEM] * 5 + [HBM] * 3,
        [VMEM] * 6,
        [jax.ShapeDtypeStruct((rows, ff), bf16), half, half]
        + [jax.ShapeDtypeStruct((rows, ff), dtype) for dtype in dtypes],
        [pltpu.VMEM((rows, ff), bf16)] * 3 + [cols, cols, pltpu.SemaphoreType.DMA((3,))],
    )(p, q, *[in_vmem(a) for a in (hid_a, hid_b, dy_late)], *got)


def tree_add(m4, m3, r1_ref, r2p_ref, r2m_ref, s4_ref, top_ref, bottom_ref):
    f32, bf16 = jnp.float32, jnp.bfloat16
    half = top_ref.shape[0]
    s3 = (m3 + r1_ref[...].astype(f32)).astype(bf16)
    top_ref[...] = s3[:half]
    bottom_ref[...] = s3[half:]
    s4_ref[...] = (m4 + r2p_ref[...].astype(f32) + r2m_ref[...].astype(f32)).astype(bf16)


def take(hbm_refs, refs, sems):
    copies = [pltpu.make_async_copy(src, dst, sems.at[j]) for j, (src, dst) in enumerate(zip(hbm_refs, refs))]
    for copy in copies:
        copy.start()
    for copy in copies:
        copy.wait()


def join_kernel(*refs):
    ins, outs, (*held, sems) = refs[:5], refs[5:8], refs[8:]
    take(ins, held, sems)
    m4_ref, m3_ref, *got = held
    tree_add(m4_ref[...], m3_ref[...], *got, *outs)


def join(m4, m3, r1, r2p, r2m, name):
    rows, ff = m4.shape
    bf16 = jnp.bfloat16
    half = jax.ShapeDtypeStruct((rows // 2, ff), bf16)
    arrays = [in_hbm(m4), in_hbm(m3), r1, r2p, r2m]
    return call(
        join_kernel,
        name,
        [HBM] * 5,
        [VMEM] * 3,
        [jax.ShapeDtypeStruct((rows, ff), bf16), half, half],
        [pltpu.VMEM((rows, ff), a.dtype) for a in arrays] + [pltpu.SemaphoreType.DMA((5,))],
    )(*arrays)


def last_hop_kernel(*refs):
    hbm, (sp_ref, sm_ref), (mp_ref, mm_ref, rp_ref, rm_ref, sems) = refs[:4], refs[4:6], refs[6:]
    f32, bf16 = jnp.float32, jnp.bfloat16
    take(hbm, (mp_ref, mm_ref, rp_ref, rm_ref), sems)
    half = rp_ref.shape[0]
    upper, lower = pl.ds(0, half), pl.ds(half, half)
    sp_ref[upper, :] = (mp_ref[upper, :].astype(f32) + rp_ref[...].astype(f32)).astype(bf16)
    sp_ref[lower, :] = mp_ref[lower, :].astype(bf16)
    sm_ref[upper, :] = mm_ref[upper, :].astype(bf16)
    sm_ref[lower, :] = (mm_ref[lower, :].astype(f32) + rm_ref[...].astype(f32)).astype(bf16)


def last_hop(mp, mm, rp, rm, name):
    out = jax.ShapeDtypeStruct(mp.shape, jnp.bfloat16)
    arrays = (mp, mm, rp, rm)
    return call(
        last_hop_kernel,
        name,
        [HBM] * 4,
        [VMEM] * 2,
        [out, out],
        [pltpu.VMEM(a.shape, a.dtype) for a in arrays] + [pltpu.SemaphoreType.DMA((4,))],
    )(*arrays)


def total_kernel(s_ref, *refs):
    (down, up), (kept_d, kept_u, other_ref) = (refs[:4], refs[4:8]), refs[8:]
    half = kept_d.shape[0]
    mine = pl.ds(pl.multiple_of(s_ref[8] * half, 16), half)
    others = pl.ds(pl.multiple_of((1 - s_ref[8]) * half, 16), half)
    for (m, *got), kept, at in ((down, kept_d, 0), (up, kept_u, half)):
        for src, dst in ((mine, kept), (others, other_ref.at[pl.ds(at, half), :])):
            got4, gotp, gotm = [r[src, :].astype(jnp.float32) for r in got]
            dst[...] = (m[src, :] + got4 + gotp + gotm).astype(dst.dtype)


def totals(scalars, down, up):
    rows, ff = down[0].shape
    half = jax.ShapeDtypeStruct((rows // 2, ff), jnp.float32)
    return call(
        total_kernel,
        "totals",
        [SMEM] + [VMEM] * 8,
        [VMEM] * 3,
        [half, half, jax.ShapeDtypeStruct((rows, ff), jnp.bfloat16)],
    )(scalars, *down, *up)


def update_kernel(s_ref, kept_d, kept_u, other_ref, noise_d, noise_u, out_d, out_u):
    half, ff = kept_d.shape
    mine = pl.ds(pl.multiple_of(s_ref[8] * ff, 128), ff)
    others = pl.ds(pl.multiple_of((1 - s_ref[8]) * ff, 128), ff)
    for at, kept, noise, out in ((0, kept_d, noise_d, out_d), (half, kept_u, noise_u, out_u)):
        out[:, mine] = (kept[...] + noise[:, mine]) * (1.0 / (2 * N_DP))
        out[:, others] = (other_ref[pl.ds(at, half), :].astype(jnp.float32) + noise[:, others]) * (1.0 / (2 * N_DP))


def updates(scalars, kept_d, kept_u, other, noise_d, noise_u):
    out = jax.ShapeDtypeStruct(noise_d.shape, jnp.float32)
    return call(update_kernel, "updates", [SMEM] + [VMEM] * 5, [VMEM] * 2, [out, out])(
        scalars, kept_d, kept_u, other, noise_d, noise_u
    )


def after(values, *earlier):
    return lax.optimization_barrier((tuple(values),) + earlier)[0]


def on_device(inputs, up_pre, gate_act, out_grad, down_weight, noise_up, noise_down):
    ff = up_pre.shape[1] // 2
    own_rows = down_weight.shape[0]
    me = lax.axis_index("dp")
    core, x, z = me % 2, (me // 2) % 2, me // 4

    def chip(dz, dx):
        return ((z + dz) % 4) * 2 + ((x + dx) % 2)

    def half_cols(a, which):
        return lax.dynamic_slice(a, (0, which * ff), (a.shape[0], ff))

    def go(a, perm):
        return lax.ppermute(a, "dp", perm)

    near_chips = [chip(0, 0), chip(3, 0), chip(1, 0), chip(0, 1), chip(2, 0)]
    far_chips = [chip(3, 1), chip(1, 1), chip(2, 1)]
    scalars = jnp.stack(near_chips + far_chips + [core]).astype(jnp.int32)

    w_mine = half_cols(down_weight, core)
    w_other = go(half_cols(down_weight, 1 - core), CORE_SWAP)
    own = jnp.where(core == 0, jnp.concatenate([w_mine, w_other]), jnp.concatenate([w_other, w_mine]))
    w_x = go(own, X_SWAP)
    w_zp = go(own, Z_DOWN)
    w_zm = go(own, Z_UP)

    dy_src, x_src = after([out_grad, inputs], own)
    dy_b = go(dy_src, CORE_SWAP)
    x_b = go(x_src, CORE_SWAP)
    x_own, dy_own = after([inputs, out_grad], own)
    xt_a, dyt_a, gx_a, gate_a, hid_a, vd_a, gu_send = prep_own(scalars, x_own, dy_own, gate_act, up_pre, ff)

    x_b, dy_b = after([x_b, dy_b], vd_a)
    xt_b, dyt_b, gx_b, gdy_b = prep_other(x_b, dy_b)

    w_x, w_zp, w_zm, gu_send = after([w_x, w_zp, w_zm, gu_send], dyt_b)
    up_half, down_half = halves(w_zm, w_zp)
    w_z2_top = go(up_half, Z_UP)
    w_z2_bot = go(down_half, Z_DOWN)
    gu_b = go(gu_send, CORE_SWAP)
    w_x = after([w_x], up_half)[0]
    w_zm_x = go(w_x, Z_UP)
    w_zp_x = go(w_x, Z_DOWN)
    near_a = near(scalars, after([dyt_a], up_half)[0], [own, w_zm, w_zp, w_x], "near_own")
    w_z2_top, w_z2_bot = after([w_z2_top, w_z2_bot], near_a)
    w_z2 = jnp.concatenate([w_z2_top, w_z2_bot])
    w_z2_x = go(w_z2, X_SWAP)
    hid_b, vd_b = hidden_other(after([gu_b], w_z2)[0], gdy_b)
    near_b = near(scalars, after([dyt_b], hid_b)[0], [own, w_zm, w_zp, w_x, w_z2], "near_other")
    w_zm_x, w_zp_x, w_z2_x = after([w_zm_x, w_zp_x, w_z2_x], near_b, vd_b)
    far_pieces = [in_hbm(w_z2), w_zm_x, w_zp_x, w_z2_x]
    act_a, act_b, part = act_grads(
        (4, 5), scalars, dyt_a, dyt_b, near_a, near_b, gate_a, gu_b, gx_a, gx_b, vd_a, vd_b, far_pieces
    )

    got = go(part, CORE_SWAP)
    part = part + jnp.concatenate([got[2:4], got[0:2], got[4:]])
    for swap in TENSOR_SWAPS[:2]:
        part = part + lax.ppermute(part, "tensor", swap)
    rest = lax.ppermute(part, "tensor", TENSOR_SWAPS[2])

    early_chips = [chip(1, 1), chip(3, 1), chip(2, 1)]
    late_chips = [chip(0, 1), chip(2, 0), chip(1, 0), chip(3, 0), chip(0, 0)]
    early = jnp.stack(early_chips).astype(jnp.int32)
    late = jnp.stack(late_chips).astype(jnp.int32)

    f32, bf16 = jnp.float32, jnp.bfloat16
    down_p, down_m, down_x = down_first(early, part, rest, dyt_a, dyt_b, hid_a, hid_b)
    d1, d2p, d2m = go(down_x, X_SWAP), go(down_p, Z_UP), go(down_m, Z_DOWN)
    act_a, act_b = after([act_a, act_b], down_x)
    up_p, up_m, up_x = up_first(early, part, rest, act_a, act_b, xt_a, xt_b)
    late = after([late], up_x)[0]
    up4, up3, up5p, up5m, up_own, hid_a, hid_b, dy_late = up_all(
        late, part, rest, act_a, act_b, xt_a, xt_b, hid_a, hid_b, dyt_a, dyt_b, [f32, f32, bf16, bf16, f32]
    )
    d1, d2p, d2m = after([d1, d2p, d2m], up_x)
    u1, u2p, u2m = go(up_x, X_SWAP), go(up_p, Z_UP), go(up_m, Z_DOWN)
    s4d, s3dt, s3db, down5p, down5m, down_own = down_later(
        part, rest, hid_a, hid_b, dy_late, (d1, d2p, d2m), [bf16, bf16, f32]
    )
    d4, d3p, d3m = go(s4d, X_SWAP), go(s3dt, Z_UP), go(s3db, Z_DOWN)
    u1, u2p, u2m = after([u1, u2p, u2m], s3dt)
    s4u, s3ut, s3ub = join(up4, up3, u1, u2p, u2m, "up_join")
    u3p, u3m, u4 = go(s3ut, Z_UP), go(s3ub, Z_DOWN), go(s4u, X_SWAP)
    d3p, d3m, d4 = after([d3p, d3m, d4], s3ut)
    s5dp, s5dm = last_hop(down5p, down5m, d3p, d3m, "down_last")
    d5p, d5m = go(s5dp, Z_UP), go(s5dm, Z_DOWN)
    u3p, u3m = after([u3p, u3m], s5dp)
    s5up, s5um = last_hop(up5p, up5m, u3p, u3m, "up_last")
    u5p, u5m = go(s5up, Z_UP), go(s5um, Z_DOWN)

    d5p, d5m, u4 = after([d5p, d5m, u4], s5up)
    kept_d, kept_u, other = totals(scalars, (down_own, d4, d5p, d5m), (up_own, u4, u5p, u5m))
    other = go(other, CORE_SWAP)
    down_update, up_update = updates(scalars, kept_d, kept_u, other, noise_down, noise_up)
    return (up_update, down_update)


def solution(mesh):
    in_specs = (
        P("dp", None),
        P("dp", "tensor"),
        P("dp", "tensor"),
        P("dp", None),
        P("dp", "tensor"),
        P("dp", "tensor"),
        P("dp", "tensor"),
    )
    out_specs = (P("dp", "tensor"), P("dp", "tensor"))
    return jax.shard_map(
        on_device, mesh=mesh, in_specs=in_specs, out_specs=out_specs, check_vma=False
    )
```
